32 devices in a mesh: src: 4 (over y, core), rcv: 8 (over z, x).
Axes of the slice: x: 2, y: 2, z: 4, core: 2. Of those that a mesh axis runs over, the one named last changes fastest.
Arguments:
- spectra: bfloat16 [256, 287, 192], P(('src', 'rcv')), may hold values from -6 to 6
- block_mask: int32 [4, 4], replicated, may hold values from 0 to 1, as said below
Outputs:
- correlations: bfloat16 [256, 4, 64, 576], P('src', None, 'rcv')
The draws below stay inside these ranges and needn't reach their ends.
Inputs may be any that keep to these rules, and one draw needn't show every extreme that they name: `block_mask`: symmetric, with ones on the diagonal.
All inputs are finite; a program needn't handle non-finite values.
Results may differ from the reference program's by a relative error of at most 0.0055.
Values may be sent and summed in bfloat16 or wider, within the bound.
No kernel may reach another device: no remote copies, remote signals or barrier semaphores. Data moves between devices by JAX's collectives and lax.ppermute only.
A program may use at most 128 MiB of HBM per device.

```python
import math
import jax
import jax.numpy as jnp
from jax import lax

BLOCK = 64
BINS = 32
SEGS = 287
BLOCKS = 4
STATIONS = 256


def draw_block_mask(key, part):
    spots = jax.random.randint(key, (BLOCKS, 2), 0, 12)
    offset = spots[:, None, :] - spots[None, :, :]
    spacing = jnp.sum(offset * offset, axis=2)
    return (spacing <= 20).astype(jnp.int32)


def block_scale(rng, dims, cuts, low, top_value):
    level, own = 1.0, jax.random.fold_in(rng, 6)
    for dim, shards_of in cuts:
        draws = jnp.exp(jax.random.uniform(jax.random.fold_in(own, dim), (shards_of,), jnp.float32, low / len(cuts), top_value / len(cuts)))
        level = level * jnp.repeat(draws, dims[dim] // shards_of).reshape([-1 if axis == dim else 1 for axis in range(len(dims))])
    return level


def noise(rng, extent, spread, bound, split=(), kind=jnp.bfloat16):
    factor_of = block_scale(rng, extent, split, -0.22, 0.18) if split else 1.0
    values = jax.random.normal(rng, extent, jnp.float32) * spread * factor_of
    return jnp.minimum(jnp.maximum(values, -bound), bound).astype(kind)


def setup_inputs(seed: int = 0) -> dict:
    streams_of = jax.random.split(jax.random.key(seed), 3)
    return {
        "spectra": noise(streams_of[0], (STATIONS, SEGS, 6 * BINS), 1.0, 6.0, ((0, 32),)),
        "block_mask": draw_block_mask(jax.random.fold_in(streams_of[2], 71), 0),
    }


def whiten(spectra):
    values = spectra.astype(jnp.float32)
    mean_power = lax.optimization_barrier(jnp.mean(values * values, axis=2, keepdims=True))
    return (values * lax.rsqrt(mean_power + 1e-06)).astype(jnp.bfloat16)

def rotate(right_rows):
    real_part = right_rows[:, :, :, 0]
    imag_part = right_rows[:, :, :, 1]
    as_real = jnp.stack([real_part, imag_part], axis=3)
    as_imag = jnp.stack([-imag_part, real_part], axis=3)
    return jnp.stack([as_real, as_imag], axis=4)

def reference(spectra, block_mask):
    whitened = whiten(spectra).reshape(STATIONS, SEGS, 3, 2, BINS)
    turned = rotate(whitened).astype(jnp.float32)
    norm_scale = 1.0 / math.sqrt(SEGS)
    block_rows = whitened.reshape(BLOCKS, BLOCK, SEGS, 3, 2, BINS)

    def per_block(inputs):
        left_rows, mask_line = inputs
        values = jnp.einsum('iwacf,jwbcef->ijabef', left_rows.astype(jnp.float32), turned, precision=lax.Precision.HIGHEST)
        values = values.reshape(BLOCK, BLOCKS, BLOCK, 18 * BINS) * norm_scale
        values = values * mask_line.astype(jnp.float32)[None, :, None, None]
        return values.astype(jnp.bfloat16)
    result = lax.map(per_block, (block_rows, block_mask))
    return result.reshape(STATIONS, BLOCKS, BLOCK, 18 * BINS)
```

```python
import functools
import math

import jax
import jax.numpy as jnp
from jax import lax
from jax.experimental import pallas as pl
from jax.experimental.pallas import tpu as pltpu
from jax.sharding import PartitionSpec as P

GROUPS = 8
TILES = 27
PAIR_ROWS = 13 * 16
GROUP_ROWS = TILES * 16
BLOCK_ROWS = GROUPS * GROUP_ROWS
HALF_ROWS = BLOCK_ROWS // 2
STATIONS = 8
F32 = jnp.float32
BF16 = jnp.bfloat16


def prepare_kernel(x_ref, first_ref, second_ref, d_ref):
    count, segs = x_ref.shape[0], x_ref.shape[1]
    tail = segs - 256
    if count < STATIONS:
        d_ref[...] = jnp.zeros_like(d_ref)
    lane_group = lax.broadcasted_iota(jnp.int32, (8, 128), 1) // 32
    for i in range(count):
        values = x_ref[i].astype(F32)
        power = jnp.mean(values * values, axis=1, keepdims=True)
        white = (values * lax.rsqrt(power + 1e-06)).astype(BF16).astype(F32)
        main = white[:256].T
        rest = jnp.concatenate([white[256:], jnp.zeros((32 - tail, 192), F32)], axis=0)
        rest = jnp.concatenate([rest] * 4, axis=0).T
        for group in range(4):
            half, pair = group // 2, group % 2
            row = pair * PAIR_ROWS + half * 8 + i
            for line in range(6):
                rows = slice(line * 32 + group * 8, line * 32 + group * 8 + 8)
                for side in range(2):
                    tile = line * 2 + side
                    d_ref[pl.ds(row + tile * 16, 8, stride=GROUP_ROWS), :] = main[
                        rows, side * 128 : side * 128 + 128
                    ]
            first = jnp.zeros((8, 128), F32)
            for line in range(4):
                rows = slice(line * 32 + group * 8, line * 32 + group * 8 + 8)
                first = jnp.where(lane_group == line, rest[rows], first)
            d_ref[pl.ds(row + 12 * 16, 8, stride=GROUP_ROWS), :] = first
        for half in range(2):
            last = jnp.zeros((8, 128), F32)
            for pair in range(2):
                for part in range(2):
                    start = (4 + part) * 32 + (half * 2 + pair) * 8
                    last = jnp.where(
                        lane_group == pair * 2 + part, rest[start : start + 8], last
                    )
            d_ref[pl.ds(26 * 16 + half * 8 + i, 8, stride=GROUP_ROWS), :] = last
    first_ref[...] = d_ref[:HALF_ROWS].astype(BF16)
    second_ref[...] = d_ref[HALF_ROWS:].astype(BF16)


def prepare(spectra):
    half = jax.ShapeDtypeStruct((HALF_ROWS, 128), BF16)
    return pl.pallas_call(
        prepare_kernel,
        out_shape=(half, half),
        scratch_shapes=[pltpu.VMEM((BLOCK_ROWS, 128), F32)],
        compiler_params=pltpu.CompilerParams(vmem_limit_bytes=48 * 2**20),
        name="prepare",
    )(spectra)


def turn_matrix():
    source = lax.broadcasted_iota(jnp.int32, (128, 1024), 0)
    column = lax.broadcasted_iota(jnp.int32, (128, 1024), 1)
    block, lane = column // 128, column % 128
    half, imag, slot = block // 4, (block // 2) % 2, block % 2
    part, seg = (lane % 64) // 32, lane % 32
    wanted = half * 64 + jnp.where(imag == 1, 1 - part, part) * 32 + seg
    sign = jnp.where((imag == 1) & (part == 1), -1.0, 1.0)
    hit = (source == wanted) & (lane // 64 == slot)
    return jnp.where(hit, sign, 0.0).astype(BF16)


def nt(left, right):
    return lax.dot_general(left, right, (((1,), (1,)), ((), ())), preferred_element_type=F32)


def products_kernel(block_count, src_count, place_ref, scale_ref, turn_ref, *refs):
    halves = refs[: 2 + 2 * block_count]
    own_ref, other_ref = refs[2 + 2 * block_count : 4 + 2 * block_count]
    left, right, sums, sems = refs[4 + 2 * block_count :]
    count = own_ref.shape[0]
    copies = [[], []]
    for h in range(2):
        rows = pl.ds(h * HALF_ROWS, HALF_ROWS)
        for n in range(block_count + 1):
            target = left.at[rows] if n == 0 else right.at[n - 1, rows]
            copy = pltpu.make_async_copy(halves[2 * n + h], target, sems.at[h, n])
            copy.start()
            copies[h].append(copy)
    lanes = block_count * 16

    def tile_of(base, tile):
        return right[:, pl.ds(base + tile * 16, 16), :].reshape(lanes, 128)

    def group(q, carry):
        base = pl.multiple_of(q * GROUP_ROWS, 16)
        turn = turn_ref[...]
        last_left = left[pl.ds(base + 26 * 16, 16), :]
        last_turned = jnp.dot(last_left, turn, preferred_element_type=F32).astype(BF16)
        last_right = tile_of(base, 26)
        for pair in range(2):
            start = base + pair * PAIR_ROWS
            tiles = [left[pl.ds(start + t * 16, 16), :] for t in range(13)]
            turned = jnp.dot(tiles[12], turn, preferred_element_type=F32).astype(BF16)
            lines = []
            for a in range(3):
                real, imag = tiles[a * 4 : a * 4 + 2], tiles[a * 4 + 2 : a * 4 + 4]
                lines.append(jnp.concatenate(real + imag, axis=1))
                lines.append(jnp.concatenate(imag + [-real[0], -real[1]], axis=1))
            main = jnp.concatenate(lines, axis=0)
            rest_right = tile_of(start, 12)
            for b in range(3):
                slot = b if b < 2 else pair
                rest = []
                for a in range(3):
                    for e in range(2):
                        of, half = (turned, a) if a < 2 else (last_turned, pair)
                        at = (half * 4 + e * 2 + slot) * 128
                        rest.append(of[:, at : at + 128])
                rest = jnp.concatenate(rest, axis=0)
                weights = jnp.concatenate([tile_of(start, b * 4 + t) for t in range(4)], axis=1)
                result = nt(main, weights) + nt(rest, rest_right if b < 2 else last_right)
                for a in range(3):
                    for e in range(2):
                        for half in range(2):
                            rows = slice((a * 2 + e) * 16 + half * 8, (a * 2 + e) * 16 + half * 8 + 8)
                            at = (a * 6 + b * 2 + e) * 32 + half * 16 + pair * 8 + q
                            for m in range(lanes // 128):
                                sums[pl.ds(m * STATIONS * 576 + at, 8, stride=576), :] = result[
                                    rows, m * 128 : m * 128 + 128
                                ]
        return carry

    for h in range(2):
        for copy in copies[h]:
            copy.wait()
        lax.fori_loop(h * (GROUPS // 2), (h + 1) * (GROUPS // 2), group, 0)

    bin_half = (lax.broadcasted_iota(jnp.int32, (8, 576), 1) % 32) < 16
    for i in range(count):
        for m in range(lanes // 128):
            start = (m * STATIONS + i) * 576
            turned = sums[start : start + 576, :].T
            for n in range(8):
                low, high = turned[n * 16 : n * 16 + 8], turned[n * 16 + 8 : n * 16 + 16]
                at = place_ref[(m * 8 + n) % src_count]
                value = (jnp.where(bin_half, low, high) * scale_ref[at]).astype(BF16)
                out = own_ref if m * 8 + n < src_count else other_ref
                out[i, at] = value[: out.shape[2]]


def products(place, scale, turn, source, blocks, count, src_count):
    out = jax.ShapeDtypeStruct((count, src_count, count, 576), BF16)
    n = len(blocks)
    smem, vmem = pl.BlockSpec(memory_space=pltpu.SMEM), pl.BlockSpec(memory_space=pltpu.VMEM)
    operands = [half for block in (source, *blocks) for half in block]
    return pl.pallas_call(
        functools.partial(products_kernel, n, src_count),
        out_shape=(out, out),
        in_specs=[smem, smem, vmem] + [pl.BlockSpec(memory_space=pl.ANY)] * len(operands),
        out_specs=(vmem, vmem),
        scratch_shapes=[
            pltpu.VMEM((BLOCK_ROWS, 128), BF16),
            pltpu.VMEM((n, BLOCK_ROWS, 128), BF16),
            pltpu.VMEM((n // 8 * STATIONS * 576, 128), F32),
            pltpu.SemaphoreType.DMA((2, n + 1)),
        ],
        compiler_params=pltpu.CompilerParams(vmem_limit_bytes=60 * 2**20),
        cost_estimate=pl.CostEstimate(
            flops=2 * 16 * 3 * 96 * 16 * n * 768, bytes_accessed=8 * 2**20, transcendentals=0
        ),
        name="products",
    )(place, scale, turn, *operands)


def on_device(spectra, block_mask):
    count, segs = spectra.shape[0], spectra.shape[1]
    src_count, rcv_count = lax.axis_size("src"), lax.axis_size("rcv")
    src, rcv = lax.axis_index("src"), lax.axis_index("rcv")
    highs, steps = src_count // 2, rcv_count // 2

    def over_core(half):
        return lax.ppermute(half, "src", [(s, s ^ 1) for s in range(src_count)])

    def over_high(half):
        return lax.ppermute(half, "src", [(s, (s + 2) % src_count) for s in range(src_count)])

    def over_x(half):
        return lax.ppermute(half, "rcv", [(r, r ^ 1) for r in range(rcv_count)])

    def over_z(half):
        return lax.ppermute(half, "rcv", [(r, (r + 2) % rcv_count) for r in range(rcv_count)])

    def each(move, block):
        return tuple(move(half) for half in block)

    scale = lax.dynamic_index_in_dim(block_mask, src, 0, keepdims=False).astype(F32) * (
        1.0 / math.sqrt(segs)
    )
    own = prepare(spectra)
    sources = [own]
    for _ in range(steps - 1):
        sources.append(each(over_z, sources[-1]))
    mine, theirs = [own], [each(over_x, own)]
    for _ in range(highs - 1):
        mine.append(each(over_high, mine[-1]))
        theirs.append((over_high(theirs[-1][0]), over_x(mine[-1][1])))
    blocks = []
    for line in (mine, theirs):
        for block in line:
            blocks += [block, each(over_core, block)]
    place = jnp.stack(
        [((src // 2 - k + highs) % highs) * 2 + lax.rem(src + c, 2) for k in range(highs) for c in range(2)]
    ).astype(jnp.int32)
    turn = turn_matrix()
    result = jnp.zeros((steps, 2, count, src_count, count, 576), BF16)
    x, z = rcv % 2, rcv // 2
    for k, source in enumerate(sources):
        kept, sent = products(place, scale, turn, source, blocks, count, src_count)
        got = over_x(sent)
        at = lax.rem(z - k + steps, steps)
        result = lax.dynamic_update_slice(result, kept[None, None], (at, x, 0, 0, 0, 0))
        result = lax.dynamic_update_slice(result, got[None, None], (at, 1 - x, 0, 0, 0, 0))
    return result.reshape(steps * 2 * count, src_count, count, 576)


def solution(mesh):
    placed = (P(("src", "rcv"), None, None), P())
    return jax.shard_map(
        on_device,
        mesh=mesh,
        in_specs=placed,
        out_specs=P("src", None, "rcv", None),
        check_vma=False,
    )
```

```python
import functools
import math

import jax
import jax.numpy as jnp
from jax import lax
from jax.experimental import pallas as pl
from jax.experimental.pallas import tpu as pltpu
from jax.sharding import PartitionSpec as P

GROUPS = 8
TILES = 27
PAIR_ROWS = 13 * 16
GROUP_ROWS = TILES * 16
BLOCK_ROWS = GROUPS * GROUP_ROWS
HALF_ROWS = BLOCK_ROWS // 2
STATIONS = 8
PACE = 40 * 2**20
F32 = jnp.float32
BF16 = jnp.bfloat16


def prepare_kernel(x_ref, whole_ref, first_ref, second_ref, d_ref):
    count, segs = x_ref.shape[0], x_ref.shape[1]
    tail = segs - 256
    if count < STATIONS:
        d_ref[...] = jnp.zeros_like(d_ref)
    lane_group = lax.broadcasted_iota(jnp.int32, (8, 128), 1) // 32
    for i in range(count):
        values = x_ref[i].astype(F32)
        power = jnp.mean(values * values, axis=1, keepdims=True)
        white = (values * lax.rsqrt(power + 1e-06)).astype(BF16).astype(F32)
        main = white[:256].T
        rest = jnp.concatenate([white[256:], jnp.zeros((32 - tail, 192), F32)], axis=0)
        rest = jnp.concatenate([rest] * 4, axis=0).T
        for group in range(4):
            half, pair = group // 2, group % 2
            row = pair * PAIR_ROWS + half * 8 + i
            for line in range(6):
                rows = slice(line * 32 + group * 8, line * 32 + group * 8 + 8)
                for side in range(2):
                    tile = line * 2 + side
                    d_ref[pl.ds(row + tile * 16, 8, stride=GROUP_ROWS), :] = main[
                        rows, side * 128 : side * 128 + 128
                    ]
            first = jnp.zeros((8, 128), F32)
            for line in range(4):
                rows = slice(line * 32 + group * 8, line * 32 + group * 8 + 8)
                first = jnp.where(lane_group == line, rest[rows], first)
            d_ref[pl.ds(row + 12 * 16, 8, stride=GROUP_ROWS), :] = first
        for half in range(2):
            last = jnp.zeros((8, 128), F32)
            for pair in range(2):
                for part in range(2):
                    start = (4 + part) * 32 + (half * 2 + pair) * 8
                    last = jnp.where(
                        lane_group == pair * 2 + part, rest[start : start + 8], last
                    )
            d_ref[pl.ds(26 * 16 + half * 8 + i, 8, stride=GROUP_ROWS), :] = last
    for h, half_ref in enumerate((first_ref, second_ref)):
        rows = slice(h * HALF_ROWS, (h + 1) * HALF_ROWS)
        value = d_ref[rows].astype(BF16)
        half_ref[...] = value
        whole_ref[rows] = value


def in_vmem(array):
    return pltpu.with_memory_space_constraint(array, pltpu.VMEM)


def prepare(spectra):
    half = jax.ShapeDtypeStruct((HALF_ROWS, 128), BF16)
    whole = jax.ShapeDtypeStruct((BLOCK_ROWS, 128), BF16)
    return pl.pallas_call(
        prepare_kernel,
        out_shape=(whole, half, half),
        scratch_shapes=[pltpu.VMEM((BLOCK_ROWS, 128), F32)],
        compiler_params=pltpu.CompilerParams(vmem_limit_bytes=16 * 2**20),
        name="prepare",
    )(spectra)


def turn_matrix():
    source = lax.broadcasted_iota(jnp.int32, (128, 1024), 0)
    column = lax.broadcasted_iota(jnp.int32, (128, 1024), 1)
    block, lane = column // 128, column % 128
    half, imag, slot = block // 4, (block // 2) % 2, block % 2
    part, seg = (lane % 64) // 32, lane % 32
    wanted = half * 64 + jnp.where(imag == 1, 1 - part, part) * 32 + seg
    sign = jnp.where((imag == 1) & (part == 1), -1.0, 1.0)
    hit = (source == wanted) & (lane // 64 == slot)
    return jnp.where(hit, sign, 0.0).astype(BF16)


def nt(left, right):
    return lax.dot_general(left, right, (((1,), (1,)), ((), ())), preferred_element_type=F32)


def products_kernel(parts, src_count, place_ref, scale_ref, turn_ref, *refs):
    operands, outs = refs[: sum(parts)], refs[sum(parts) : sum(parts) + 2]
    own_ref, other_ref = outs
    sums, turned_ref = refs[sum(parts) + 2 :]
    count = own_ref.shape[0]
    block_count = len(parts) - 1
    lanes = block_count * 16
    pieces = []
    for n in parts:
        of, operands = operands[:n], operands[n:]
        pieces.append([(of[h], 0) if n == 2 else (of[0], h * HALF_ROWS) for h in range(2)])

    for h in range(2):
        left, offset = pieces[0][h]
        steps = GROUPS // 2
        tails = []
        for q in range(steps):
            for tile in (12, 25, 26):
                start = offset + q * GROUP_ROWS + tile * 16
                tails.append(left[start : start + 16, :])
        turned_ref[...] = jnp.dot(
            jnp.concatenate(tails, axis=0), turn_ref[...], preferred_element_type=F32
        ).astype(BF16)
        for q in range(steps):

            def tile_of(tile):
                start = q * GROUP_ROWS + tile * 16
                return jnp.concatenate(
                    [ref[at + start : at + start + 16, :] for ref, at in (p[h] for p in pieces[1:])],
                    axis=0,
                )

            last_right = tile_of(26)
            for pair in range(2):
                base = offset + q * GROUP_ROWS + pair * PAIR_ROWS
                tiles = [left[base + t * 16 : base + t * 16 + 16, :] for t in range(12)]
                lines = []
                for a in range(3):
                    real, imag = tiles[a * 4 : a * 4 + 2], tiles[a * 4 + 2 : a * 4 + 4]
                    lines.append(jnp.concatenate(real + imag, axis=1))
                    lines.append(jnp.concatenate(imag + [-real[0], -real[1]], axis=1))
                main = jnp.concatenate(lines, axis=0)
                rest_right = tile_of(pair * 13 + 12)
                for b in range(3):
                    slot = b if b < 2 else pair
                    rest = []
                    for a in range(3):
                        row, half = (q * 3 + pair, a) if a < 2 else (q * 3 + 2, pair)
                        for e in range(2):
                            at = (half * 4 + e * 2 + slot) * 128
                            rest.append(turned_ref[row * 16 : row * 16 + 16, at : at + 128])
                    rest = jnp.concatenate(rest, axis=0)
                    weights = [tile_of(pair * 13 + b * 4 + t) for t in range(4)]
                    weights.append(rest_right if b < 2 else last_right)
                    result = nt(
                        jnp.concatenate([main, rest], axis=1), jnp.concatenate(weights, axis=1)
                    )
                    for a in range(3):
                        for e in range(2):
                            for half in range(2):
                                row = (a * 2 + e) * 16 + half * 8
                                bin_ = half * 16 + pair * 8 + h * steps + q
                                at = (a * 6 + b * 2 + e) * 32 + bin_
                                for m in range(lanes // 128):
                                    sums[
                                        pl.ds(m * STATIONS * 576 + at, 8, stride=576), :
                                    ] = result[row : row + 8, m * 128 : m * 128 + 128]

    bin_half = (lax.broadcasted_iota(jnp.int32, (8, 576), 1) % 32) < 16
    for i in range(count):
        for m in range(lanes // 128):
            start = (m * STATIONS + i) * 576
            turned = sums[start : start + 576, :].T
            for n in range(8):
                low, high = turned[n * 16 : n * 16 + 8], turned[n * 16 + 8 : n * 16 + 16]
                at = place_ref[(m * 8 + n) % src_count]
                value = (jnp.where(bin_half, low, high) * scale_ref[at]).astype(BF16)
                out = own_ref if m * 8 + n < src_count else other_ref
                out[i, at] = value[: out.shape[2]]


def products(place, scale, turn, source, blocks, count, src_count):
    out = jax.ShapeDtypeStruct((count, src_count, count, 576), BF16)
    n = len(blocks)
    parts = tuple(len(block) for block in (source, *blocks))
    smem, vmem = pl.BlockSpec(memory_space=pltpu.SMEM), pl.BlockSpec(memory_space=pltpu.VMEM)
    operands = [in_vmem(piece) for block in (source, *blocks) for piece in block]
    return pl.pallas_call(
        functools.partial(products_kernel, parts, src_count),
        out_shape=(out, out),
        in_specs=[smem, smem, vmem] + [vmem] * len(operands),
        out_specs=(vmem, vmem),
        scratch_shapes=[
            pltpu.VMEM((n // 8 * STATIONS * 576, 128), F32),
            pltpu.VMEM((GROUPS // 2 * 3 * 16, 1024), BF16),
        ],
        compiler_params=pltpu.CompilerParams(vmem_limit_bytes=24 * 2**20),
        cost_estimate=pl.CostEstimate(
            flops=2 * 16 * 3 * 96 * 16 * n * 768, bytes_accessed=8 * 2**20, transcendentals=0
        ),
        name="products",
    )(place, scale, turn, *operands)


def paced(array):
    return pl.pallas_call(
        lambda x_ref, o_ref: None,
        out_shape=jax.ShapeDtypeStruct(array.shape, array.dtype),
        in_specs=[pl.BlockSpec(memory_space=pl.ANY)],
        out_specs=pl.BlockSpec(memory_space=pl.ANY),
        input_output_aliases={0: 0},
        cost_estimate=pl.CostEstimate(flops=0, bytes_accessed=PACE, transcendentals=0),
        name="paced",
    )(array)


def on_device(spectra, block_mask):
    count, segs = spectra.shape[0], spectra.shape[1]
    src_count, rcv_count = lax.axis_size("src"), lax.axis_size("rcv")
    src, rcv = lax.axis_index("src"), lax.axis_index("rcv")
    highs, steps = src_count // 2, rcv_count // 2

    def over_core(half):
        return lax.ppermute(half, "src", [(s, s ^ 1) for s in range(src_count)])

    def over_high(half):
        return lax.ppermute(half, "src", [(s, (s + 2) % src_count) for s in range(src_count)])

    def over_x(half):
        return lax.ppermute(half, "rcv", [(r, r ^ 1) for r in range(rcv_count)])

    def over_z(half):
        return lax.ppermute(half, "rcv", [(r, (r + 2) % rcv_count) for r in range(rcv_count)])

    scale = lax.dynamic_index_in_dim(block_mask, src, 0, keepdims=False).astype(F32) * (
        1.0 / math.sqrt(segs)
    )
    whole, *halves = prepare(spectra)
    sources = [halves]
    for k in range(steps - 1):
        pace = paced if k < steps - 2 else (lambda half: half)
        sources.append([pace(over_z(half)) for half in sources[-1]])
    high, beside = whole, over_x(whole)
    mine, theirs = [(high,)], [(beside,)]
    for _ in range(highs - 1):
        first = beside[:HALF_ROWS]
        high, first = lax.optimization_barrier((over_high(high), first))
        beside = over_high(first)
        mine.append((high,))
        theirs.append((beside, over_x(high[HALF_ROWS:])))
    blocks = []
    for line in (mine, theirs):
        for block in line:
            blocks += [block, tuple(over_core(piece) for piece in block)]
    place = jnp.stack(
        [((src // 2 - k + highs) % highs) * 2 + lax.rem(src + c, 2) for k in range(highs) for c in range(2)]
    ).astype(jnp.int32)
    turn = turn_matrix()
    result = jnp.zeros((steps, 2, count, src_count, count, 576), BF16)
    x, z = rcv % 2, rcv // 2
    for k, source in enumerate(sources):
        kept, sent = products(place, scale, turn, source, blocks, count, src_count)
        got = over_x(sent)
        at = lax.rem(z - k + steps, steps)
        result = lax.dynamic_update_slice(result, kept[None, None], (at, x, 0, 0, 0, 0))
        result = lax.dynamic_update_slice(result, got[None, None], (at, 1 - x, 0, 0, 0, 0))
    return result.reshape(steps * 2 * count, src_count, count, 576)


def solution(mesh):
    placed = (P(("src", "rcv"), None, None), P())
    return jax.shard_map(
        on_device,
        mesh=mesh,
        in_specs=placed,
        out_specs=P("src", None, "rcv", None),
        check_vma=False,
    )
```

```python
import functools
import math

import jax
import jax.numpy as jnp
import numpy as np
from jax import lax
from jax.experimental import pallas as pl
from jax.experimental.pallas import tpu as pltpu
from jax.sharding import PartitionSpec as P

GROUPS = 8
TILES = 27
PAIR_ROWS = 13 * 16
GROUP_ROWS = TILES * 16
BLOCK_ROWS = GROUPS * GROUP_ROWS
HALF_ROWS = BLOCK_ROWS // 2
STATIONS = 8
CUTS = (0, 4, 8)
PACE = 80 * 2**20
F32 = jnp.float32
BF16 = jnp.bfloat16


def prepare_kernel(x_ref, whole_ref, d_ref):
    count, segs = x_ref.shape[0], x_ref.shape[1]
    tail = segs - 256
    if count < STATIONS:
        d_ref[...] = jnp.zeros_like(d_ref)
    lane_group = lax.broadcasted_iota(jnp.int32, (8, 128), 1) // 32
    for i in range(count):
        values = x_ref[i].astype(F32)
        power = jnp.mean(values * values, axis=1, keepdims=True)
        white = (values * lax.rsqrt(power + 1e-06)).astype(BF16).astype(F32)
        main = white[:256].T
        rest = jnp.concatenate([white[256:], jnp.zeros((32 - tail, 192), F32)], axis=0)
        rest = jnp.concatenate([rest] * 4, axis=0).T
        for group in range(4):
            half, pair = group // 2, group % 2
            row = pair * PAIR_ROWS + half * 8 + i
            for line in range(6):
                rows = slice(line * 32 + group * 8, line * 32 + group * 8 + 8)
                for side in range(2):
                    tile = line * 2 + side
                    d_ref[pl.ds(row + tile * 16, 8, stride=GROUP_ROWS), :] = main[
                        rows, side * 128 : side * 128 + 128
                    ]
            first = jnp.zeros((8, 128), F32)
            for line in range(4):
                rows = slice(line * 32 + group * 8, line * 32 + group * 8 + 8)
                first = jnp.where(lane_group == line, rest[rows], first)
            d_ref[pl.ds(row + 12 * 16, 8, stride=GROUP_ROWS), :] = first
        for half in range(2):
            last = jnp.zeros((8, 128), F32)
            for pair in range(2):
                for part in range(2):
                    start = (4 + part) * 32 + (half * 2 + pair) * 8
                    last = jnp.where(
                        lane_group == pair * 2 + part, rest[start : start + 8], last
                    )
            d_ref[pl.ds(26 * 16 + half * 8 + i, 8, stride=GROUP_ROWS), :] = last
    for start in range(0, BLOCK_ROWS, 144):
        whole_ref[start : start + 144] = d_ref[start : start + 144].astype(BF16)


def in_vmem(array):
    return pltpu.with_memory_space_constraint(array, pltpu.VMEM)


def prepare(spectra):
    vmem = pl.BlockSpec(memory_space=pltpu.VMEM)
    return pl.pallas_call(
        prepare_kernel,
        out_shape=pltpu.VMEM((BLOCK_ROWS, 128), BF16),
        in_specs=[vmem],
        out_specs=vmem,
        scratch_shapes=[pltpu.VMEM((BLOCK_ROWS, 128), F32)],
        compiler_params=pltpu.CompilerParams(vmem_limit_bytes=8 * 2**20),
        name="prepare",
    )(spectra)


def turn_matrix():
    lane = np.arange(128)
    late, imag = lane // 64, lane // 32 % 2
    lines = np.stack([late == 0, late == 1, imag == 0, -imag]).astype(np.float32)
    return jnp.asarray(np.repeat(lines, 16, axis=0), BF16)


def nt(left, right):
    return lax.dot_general(left, right, (((1,), (1,)), ((), ())), preferred_element_type=F32)


def products_kernel(layout, source_count, src_count, norm, mask_ref, turn_ref, *refs):
    arrays = 1 + max(n for block in layout for n, _ in block)
    operands, outs, (token_ref, sums) = refs[:arrays], refs[arrays:-2], refs[-2:]
    token_ref[...] = jnp.zeros_like(token_ref)
    count = outs[0].shape[0]
    block_count = len(layout) - source_count
    lanes = block_count * 16
    tiles_wide = sums.shape[0] // (source_count * STATIONS * 576)
    pieces = [[(operands[n], at) for n, at in block] for block in layout]
    lefts, rights = pieces[:source_count], pieces[source_count:]
    steps = GROUPS // 2
    for h in range(2):
        def group(q, carry, h=h):
            def rows_of(ref, at, tile):
                return ref[pl.ds(pl.multiple_of(q * GROUP_ROWS + at + tile * 16, 16), 16), :]

            def tile_of(tile):
                return jnp.concatenate([rows_of(*p[h], tile) for p in rights], axis=0)

            def turned(tile):
                swapped = pltpu.roll(tile, 96, 1) * signs[2] + pltpu.roll(tile, 32, 1) * signs[3]
                lines = []
                for value in (tile, swapped):
                    across = pltpu.roll(value, 64, 1)
                    lines.append((value * signs[0], across * signs[1], across * signs[0], value * signs[1]))
                return [[line[2 * half : 2 * half + 2] for line in lines] for half in range(2)]

            signs = [turn_ref[16 * k : 16 * k + 16] for k in range(4)]
            last_right = tile_of(26)
            last_turned = [turned(rows_of(*p[h], 26)) for p in lefts]
            for pair in range(2):
                lines = []
                for p in lefts:
                    tiles = [rows_of(*p[h], pair * 13 + t) for t in range(12)]
                    for a in range(3):
                        real, imag = tiles[a * 4 : a * 4 + 2], tiles[a * 4 + 2 : a * 4 + 4]
                        lines.append(jnp.concatenate(real + imag, axis=1))
                        lines.append(jnp.concatenate(imag + [-real[0], -real[1]], axis=1))
                main = jnp.concatenate(lines, axis=0)
                rest_right = tile_of(pair * 13 + 12)
                first_turned = [turned(rows_of(*p[h], pair * 13 + 12)) for p in lefts]
                for b in range(3):
                    slot = b if b < 2 else pair
                    rest = []
                    for source in range(source_count):
                        for a in range(3):
                            of = first_turned[source][a] if a < 2 else last_turned[source][pair]
                            rest += [of[e][slot] for e in range(2)]
                    rest = jnp.concatenate(rest, axis=0)
                    weights = [tile_of(pair * 13 + b * 4 + t) for t in range(4)]
                    weights.append(rest_right if b < 2 else last_right)
                    result = nt(
                        jnp.concatenate([main, rest], axis=1), jnp.concatenate(weights, axis=1)
                    )
                    for n in range(source_count * 12):
                        source, a, e, half = n // 12, n // 4 % 3, n // 2 % 2, n % 2
                        at = (a * 6 + b * 2 + e) * 32 + half * 16 + pair * 8 + h * steps
                        for m in range(tiles_wide):
                            start = (source * tiles_wide + m) * STATIONS * 576 + at + q
                            wide = min(128, lanes)
                            sums[pl.ds(start, 8, stride=576), :wide] = result[
                                n * 8 : n * 8 + 8, m * 128 : m * 128 + wide
                            ]
            return carry

        lax.fori_loop(0, steps, group, 0, unroll=block_count <= 8)

    src = lax.axis_index("src")
    highs = src_count // 2
    places, scales = [], []
    for block in range(src_count):
        high = lax.rem(src // 2 + highs - block // 2, highs)
        places.append(high * 2 + lax.rem(src + block, 2))
        scales.append(mask_ref[src, places[-1]].astype(F32) * norm)

    bin_half = (lax.broadcasted_iota(jnp.int32, (8, 576), 1) % 32) < 16
    for source in range(source_count):
        for i in range(count):
            for m in range(tiles_wide):
                start = ((source * tiles_wide + m) * STATIONS + i) * 576
                turned = sums[start : start + 576, :].T
                for n in range(min(8, block_count)):
                    low, high = turned[n * 16 : n * 16 + 8], turned[n * 16 + 8 : n * 16 + 16]
                    which, block = divmod(m * 8 + n, src_count)
                    at = places[block]
                    value = (jnp.where(bin_half, low, high) * scales[block]).astype(BF16)
                    outs[2 * source + which][i, at] = value[: outs[0].shape[2]]


@functools.partial(jax.jit, static_argnums=(3, 4, 5, 6))
def products_of(mask, turn, operands, layout, s, count, norm):
    n = len(layout) - s
    src_count = n // 2
    sum_rows = s * ((n + 7) // 8) * STATIONS * 576
    out = jax.ShapeDtypeStruct((count, src_count, count, 576), BF16)
    smem, vmem = pl.BlockSpec(memory_space=pltpu.SMEM), pl.BlockSpec(memory_space=pltpu.VMEM)
    operands = [in_vmem(operand) for operand in operands]
    return pl.pallas_call(
        functools.partial(products_kernel, layout, s, src_count, norm),
        out_shape=(out,) * (2 * s) + (jax.ShapeDtypeStruct((8, 128), F32),),
        in_specs=[smem, vmem] + [vmem] * len(operands),
        out_specs=(vmem,) * (2 * s + 1),
        scratch_shapes=[pltpu.VMEM((sum_rows, 128), F32)],
        compiler_params=pltpu.CompilerParams(vmem_limit_bytes=2 * sum_rows // s * 512 + 12 * 2**20),
        cost_estimate=pl.CostEstimate(
            flops=2 * 16 * 3 * 96 * s * 16 * n * 768, bytes_accessed=8 * 2**20, transcendentals=0
        ),
        name="products",
    )(mask, turn, *operands)


def products(mask, turn, sources, blocks, count, norm):
    operands, layout = [], []
    for block in (*sources, *blocks):
        layout.append([])
        for array, at in block:
            known = [n for n, operand in enumerate(operands) if operand is array]
            layout[-1].append((known[0] if known else len(operands), at))
            if not known:
                operands.append(array)
    layout = tuple(map(tuple, layout))
    return products_of(mask, turn, operands, layout, len(sources), count, norm)


def paced(array, after=(), wait_bytes=0):
    any_ = pl.BlockSpec(memory_space=pl.ANY)
    return pl.pallas_call(
        lambda *refs: None,
        out_shape=pltpu.VMEM(array.shape, array.dtype),
        in_specs=[any_] * (1 + len(after)),
        out_specs=any_,
        input_output_aliases={0: 0},
        cost_estimate=pl.CostEstimate(flops=0, bytes_accessed=wait_bytes, transcendentals=0),
        compiler_params=pltpu.CompilerParams(vmem_limit_bytes=2**20),
        name="paced",
    )(in_vmem(array), *after)


def rearranged(arrays, outputs, after=()):
    def kernel(*refs):
        ins, outs = refs[: len(arrays)], refs[len(arrays) + len(after) :]
        for out_ref, pieces in zip(outs, outputs):
            at = 0
            for array, start, rows in pieces:
                for row in range(0, rows, 144):
                    out_ref[at + row : at + row + 144] = ins[array][start + row : start + row + 144]
                at += rows

    vmem = pl.BlockSpec(memory_space=pltpu.VMEM)
    sizes = [sum(rows for _, _, rows in pieces) for pieces in outputs]
    total = sum(sizes) + sum(array.shape[0] for array in arrays)
    return pl.pallas_call(
        kernel,
        out_shape=tuple(pltpu.VMEM((size, 128), BF16) for size in sizes),
        in_specs=[vmem] * len(arrays) + [pl.BlockSpec(memory_space=pl.ANY)] * len(after),
        out_specs=(vmem,) * len(outputs),
        compiler_params=pltpu.CompilerParams(vmem_limit_bytes=total * 256 + 2 * 2**20),
        name="rearranged",
    )(*map(in_vmem, arrays), *after)


def blank(shape, token):
    return pl.pallas_call(
        lambda token_ref, o_ref: None,
        out_shape=pltpu.HBM(shape, BF16),
        in_specs=[pl.BlockSpec(memory_space=pl.ANY)],
        out_specs=pl.BlockSpec(memory_space=pltpu.HBM),
        compiler_params=pltpu.CompilerParams(vmem_limit_bytes=2**20),
        name="blank",
    )(token)


def on_device(spectra, block_mask):
    count, segs = spectra.shape[0], spectra.shape[1]
    src_count, rcv_count = lax.axis_size("src"), lax.axis_size("rcv")
    src, rcv = lax.axis_index("src"), lax.axis_index("rcv")
    highs, steps = src_count // 2, rcv_count // 2

    def over_core(half):
        return lax.ppermute(half, "src", [(s, s ^ 1) for s in range(src_count)])

    def over_high(half):
        return lax.ppermute(half, "src", [(s, (s + 2) % src_count) for s in range(src_count)])

    def over_x(half):
        return lax.ppermute(half, "rcv", [(r, r ^ 1) for r in range(rcv_count)])

    def over_z(half):
        return lax.ppermute(half, "rcv", [(r, (r + 2) % rcv_count) for r in range(rcv_count)])

    def whole_at(array, start=0):
        return (array, start), (array, start + HALF_ROWS)

    own = prepare(spectra)
    passing = paced(over_z(own), wait_bytes=PACE)
    sources = [whole_at(own), whole_at(passing)]
    beside, high = over_x(own), over_high(own)
    cuts, ahead = [n * GROUP_ROWS for n in CUTS], []
    if steps > 2:
        listed = [[(0, start, end - start)] for start, end in zip(cuts, cuts[1:])]
        ahead = [over_z(piece) for piece in rearranged([passing], listed)]
    mine, theirs = [whole_at(own)], [whole_at(beside)]
    if highs > 1:
        three = [(n, 0, BLOCK_ROWS) for n in range(3)]
        joined, first, second = rearranged(
            [own, beside, high],
            [three, [(1, 0, HALF_ROWS)], [(2, HALF_ROWS, HALF_ROWS)]],
            (passing,),
        )
        joined = over_core(joined)
        mine += [whole_at(joined), whole_at(high), whole_at(joined, 2 * BLOCK_ROWS)]
        theirs += [whole_at(joined, BLOCK_ROWS)]
    else:
        mine += [whole_at(over_core(own))]
        theirs += [whole_at(over_core(beside))]
    for k in range(1, highs):
        if k > 1:
            high = over_high(high)
            (second,) = rearranged([high], [[(0, HALF_ROWS, HALF_ROWS)]])
            mine += [whole_at(high), whole_at(over_core(high))]
        first, across = over_high(first), over_x(second)
        (pair,) = rearranged(
            [first, across], [[(0, 0, HALF_ROWS), (1, 0, HALF_ROWS)]], ahead[:1] if k == 1 else ()
        )
        theirs += [((first, 0), (across, 0)), whole_at(over_core(pair))]
    blocks = mine + theirs
    if len(blocks) <= 8:
        arrays, listed = [], []
        for block in blocks:
            for array, at in block:
                if not any(array is known for known in arrays):
                    arrays.append(array)
                listed.append(([array is known for known in arrays].index(True), at, HALF_ROWS))
        (together,) = rearranged(arrays, [listed], ahead[1:-1])
        blocks = [whole_at(together, n * BLOCK_ROWS) for n in range(len(blocks))]
    held = list({id(array): array for block in blocks for array, _ in block}.values())
    turn = turn_matrix()
    x, z = rcv % 2, rcv // 2
    pieces = []
    for k in range(1, steps):
        batch = sources
        if k + 1 < steps:
            early, late = ahead if k == 1 else (over_z(early), over_z(late))
        *outs, token = products(block_mask, turn, batch, blocks, count, 1.0 / math.sqrt(segs))
        if k + 2 < steps:
            late = paced(late, (token,), PACE)
        sources = [((early, 0), (late, 0))]
        pieces += [(kept, over_x(sent)) for kept, sent in zip(outs[::2], outs[1::2])]
    result = blank((steps, 2, count, src_count, count, 576), token)
    for k, (kept, got) in enumerate(pieces):
        at = lax.rem(z - k + steps, steps)
        result = lax.dynamic_update_slice(result, kept[None, None], (at, x, 0, 0, 0, 0))
        result = lax.dynamic_update_slice(result, got[None, None], (at, 1 - x, 0, 0, 0, 0))
    return result.reshape(steps * 2 * count, src_count, count, 576)


def solution(mesh):
    placed = (P(("src", "rcv"), None, None), P())
    return jax.shard_map(
        on_device,
        mesh=mesh,
        in_specs=placed,
        out_specs=P("src", None, "rcv", None),
        check_vma=False,
    )
```

```python
import functools
import math

import jax
import jax.numpy as jnp
import numpy as np
from jax import lax
from jax.experimental import pallas as pl
from jax.experimental.pallas import tpu as pltpu
from jax.sharding import PartitionSpec as P

GROUPS = 8
TILES = 27
PAIR_ROWS = 13 * 16
GROUP_ROWS = TILES * 16
BLOCK_ROWS = GROUPS * GROUP_ROWS
HALF_ROWS = BLOCK_ROWS // 2
STATIONS = 8
CUTS = (0, 5, 8)
PACE = 80 * 2**20
F32 = jnp.float32
BF16 = jnp.bfloat16


def prepare_kernel(x_ref, whole_ref, d_ref):
    count, segs = x_ref.shape[0], x_ref.shape[1]
    tail = segs - 256
    if count < STATIONS:
        d_ref[...] = jnp.zeros_like(d_ref)
    lane_group = lax.broadcasted_iota(jnp.int32, (8, 128), 1) // 32
    for i in range(count):
        values = x_ref[i].astype(F32)
        power = jnp.mean(values * values, axis=1, keepdims=True)
        white = (values * lax.rsqrt(power + 1e-06)).astype(BF16).astype(F32)
        main = white[:256].T
        rest = jnp.concatenate([white[256:], jnp.zeros((32 - tail, 192), F32)], axis=0)
        rest = jnp.concatenate([rest] * 4, axis=0).T
        for group in range(4):
            half, pair = group // 2, group % 2
            row = pair * PAIR_ROWS + half * 8 + i
            for line in range(6):
                rows = slice(line * 32 + group * 8, line * 32 + group * 8 + 8)
                for side in range(2):
                    tile = line * 2 + side
                    d_ref[pl.ds(row + tile * 16, 8, stride=GROUP_ROWS), :] = main[
                        rows, side * 128 : side * 128 + 128
                    ]
            first = jnp.zeros((8, 128), F32)
            for line in range(4):
                rows = slice(line * 32 + group * 8, line * 32 + group * 8 + 8)
                first = jnp.where(lane_group == line, rest[rows], first)
            d_ref[pl.ds(row + 12 * 16, 8, stride=GROUP_ROWS), :] = first
        for half in range(2):
            last = jnp.zeros((8, 128), F32)
            for pair in range(2):
                for part in range(2):
                    start = (4 + part) * 32 + (half * 2 + pair) * 8
                    last = jnp.where(
                        lane_group == pair * 2 + part, rest[start : start + 8], last
                    )
            d_ref[pl.ds(26 * 16 + half * 8 + i, 8, stride=GROUP_ROWS), :] = last
    for start in range(0, BLOCK_ROWS, 144):
        whole_ref[start : start + 144] = d_ref[start : start + 144].astype(BF16)


def in_vmem(array):
    return pltpu.with_memory_space_constraint(array, pltpu.VMEM)


def prepare(spectra):
    vmem = pl.BlockSpec(memory_space=pltpu.VMEM)
    return pl.pallas_call(
        prepare_kernel,
        out_shape=pltpu.VMEM((BLOCK_ROWS, 128), BF16),
        in_specs=[vmem],
        out_specs=vmem,
        scratch_shapes=[pltpu.VMEM((BLOCK_ROWS, 128), F32)],
        compiler_params=pltpu.CompilerParams(vmem_limit_bytes=8 * 2**20),
        name="prepare",
    )(spectra)


def turn_matrix():
    lane = np.arange(128)
    late, imag = lane // 64, lane // 32 % 2
    lines = np.stack([late == 0, late == 1, imag == 0, -imag]).astype(np.float32)
    return jnp.asarray(np.repeat(lines, 16, axis=0), BF16)


def nt(left, right):
    return lax.dot_general(left, right, (((1,), (1,)), ((), ())), preferred_element_type=F32)


def products_kernel(layout, source_count, src_count, norm, mask_ref, turn_ref, *refs):
    arrays = 1 + max(n for block in layout for n, _ in block)
    operands, outs, (token_ref, sums) = refs[:arrays], refs[arrays:-2], refs[-2:]
    token_ref[...] = jnp.zeros_like(token_ref)
    count = outs[0].shape[0]
    block_count = len(layout) - source_count
    lanes = block_count * 16
    tiles_wide = sums.shape[0] // (source_count * STATIONS * 576)
    pieces = [[(operands[n], at) for n, at in block] for block in layout]
    lefts, rights = pieces[:source_count], pieces[source_count:]
    steps = GROUPS // 2
    for h in range(2):
        def group(q, carry, h=h):
            def rows_of(ref, at, tile):
                return ref[pl.ds(pl.multiple_of(q * GROUP_ROWS + at + tile * 16, 16), 16), :]

            def tile_of(tile):
                return jnp.concatenate([rows_of(*p[h], tile) for p in rights], axis=0)

            def turned(tile):
                swapped = pltpu.roll(tile, 96, 1) * signs[2] + pltpu.roll(tile, 32, 1) * signs[3]
                lines = []
                for value in (tile, swapped):
                    across = pltpu.roll(value, 64, 1)
                    lines.append((value * signs[0], across * signs[1], across * signs[0], value * signs[1]))
                return [[line[2 * half : 2 * half + 2] for line in lines] for half in range(2)]

            signs = [turn_ref[16 * k : 16 * k + 16] for k in range(4)]
            last_right = tile_of(26)
            last_turned = [turned(rows_of(*p[h], 26)) for p in lefts]
            for pair in range(2):
                lines = []
                for p in lefts:
                    tiles = [rows_of(*p[h], pair * 13 + t) for t in range(12)]
                    for a in range(3):
                        real, imag = tiles[a * 4 : a * 4 + 2], tiles[a * 4 + 2 : a * 4 + 4]
                        lines.append(jnp.concatenate(real + imag, axis=1))
                        lines.append(jnp.concatenate(imag + [-real[0], -real[1]], axis=1))
                main = jnp.concatenate(lines, axis=0)
                rest_right = tile_of(pair * 13 + 12)
                first_turned = [turned(rows_of(*p[h], pair * 13 + 12)) for p in lefts]
                for b in range(3):
                    slot = b if b < 2 else pair
                    rest = []
                    for source in range(source_count):
                        for a in range(3):
                            of = first_turned[source][a] if a < 2 else last_turned[source][pair]
                            rest += [of[e][slot] for e in range(2)]
                    rest = jnp.concatenate(rest, axis=0)
                    weights = [tile_of(pair * 13 + b * 4 + t) for t in range(4)]
                    weights.append(rest_right if b < 2 else last_right)
                    result = nt(
                        jnp.concatenate([main, rest], axis=1), jnp.concatenate(weights, axis=1)
                    )
                    for n in range(source_count * 12):
                        source, a, e, half = n // 12, n // 4 % 3, n // 2 % 2, n % 2
                        at = (a * 6 + b * 2 + e) * 32 + half * 16 + pair * 8 + h * steps
                        for m in range(tiles_wide):
                            start = (source * tiles_wide + m) * STATIONS * 576 + at + q
                            wide = min(128, lanes)
                            sums[pl.ds(start, 8, stride=576), :wide] = result[
                                n * 8 : n * 8 + 8, m * 128 : m * 128 + wide
                            ]
            return carry

        lax.fori_loop(0, steps, group, 0, unroll=block_count <= 8)

    src = lax.axis_index("src")
    highs = src_count // 2
    places, scales = [], []
    for block in range(src_count):
        high = lax.rem(src // 2 + highs - block // 2, highs)
        places.append(high * 2 + lax.rem(src + block, 2))
        scales.append(mask_ref[src, places[-1]].astype(F32) * norm)

    bin_half = (lax.broadcasted_iota(jnp.int32, (8, 576), 1) % 32) < 16
    for source in range(source_count):
        for i in range(count):
            for m in range(tiles_wide):
                start = ((source * tiles_wide + m) * STATIONS + i) * 576
                turned = sums[start : start + 576, :].T
                for n in range(min(8, block_count)):
                    low, high = turned[n * 16 : n * 16 + 8], turned[n * 16 + 8 : n * 16 + 16]
                    which, block = divmod(m * 8 + n, src_count)
                    at = places[block]
                    value = (jnp.where(bin_half, low, high) * scales[block]).astype(BF16)
                    outs[2 * source + which][i, at] = value[: outs[0].shape[2]]


@functools.partial(jax.jit, static_argnums=(3, 4, 5, 6))
def products_of(mask, turn, operands, layout, s, count, norm):
    n = len(layout) - s
    src_count = n // 2
    sum_rows = s * ((n + 7) // 8) * STATIONS * 576
    out = jax.ShapeDtypeStruct((count, src_count, count, 576), BF16)
    smem, vmem = pl.BlockSpec(memory_space=pltpu.SMEM), pl.BlockSpec(memory_space=pltpu.VMEM)
    operands = [in_vmem(operand) for operand in operands]
    return pl.pallas_call(
        functools.partial(products_kernel, layout, s, src_count, norm),
        out_shape=(out,) * (2 * s) + (jax.ShapeDtypeStruct((8, 128), F32),),
        in_specs=[smem, vmem] + [vmem] * len(operands),
        out_specs=(vmem,) * (2 * s + 1),
        scratch_shapes=[pltpu.VMEM((sum_rows, 128), F32)],
        compiler_params=pltpu.CompilerParams(vmem_limit_bytes=2 * sum_rows // s * 512 + 12 * 2**20),
        cost_estimate=pl.CostEstimate(
            flops=2 * 16 * 3 * 96 * s * 16 * n * 768, bytes_accessed=8 * 2**20, transcendentals=0
        ),
        name="products",
    )(mask, turn, *operands)


def products(mask, turn, sources, blocks, count, norm):
    operands, layout = [], []
    for block in (*sources, *blocks):
        layout.append([])
        for array, at in block:
            known = [n for n, operand in enumerate(operands) if operand is array]
            layout[-1].append((known[0] if known else len(operands), at))
            if not known:
                operands.append(array)
    layout = tuple(map(tuple, layout))
    return products_of(mask, turn, operands, layout, len(sources), count, norm)


def paced(array, after=(), wait_bytes=0):
    any_ = pl.BlockSpec(memory_space=pl.ANY)
    return pl.pallas_call(
        lambda *refs: None,
        out_shape=pltpu.VMEM(array.shape, array.dtype),
        in_specs=[any_] * (1 + len(after)),
        out_specs=any_,
        input_output_aliases={0: 0},
        cost_estimate=pl.CostEstimate(flops=0, bytes_accessed=wait_bytes, transcendentals=0),
        compiler_params=pltpu.CompilerParams(vmem_limit_bytes=2**20),
        name="paced",
    )(in_vmem(array), *after)


def rearranged(arrays, outputs, after=()):
    def kernel(*refs):
        ins, outs = refs[: len(arrays)], refs[len(arrays) + len(after) :]
        for out_ref, pieces in zip(outs, outputs):
            at = 0
            for array, start, rows in pieces:
                for row in range(0, rows, 144):
                    out_ref[at + row : at + row + 144] = ins[array][start + row : start + row + 144]
                at += rows

    vmem = pl.BlockSpec(memory_space=pltpu.VMEM)
    sizes = [sum(rows for _, _, rows in pieces) for pieces in outputs]
    total = sum(sizes) + sum(array.shape[0] for array in arrays)
    return pl.pallas_call(
        kernel,
        out_shape=tuple(pltpu.VMEM((size, 128), BF16) for size in sizes),
        in_specs=[vmem] * len(arrays) + [pl.BlockSpec(memory_space=pl.ANY)] * len(after),
        out_specs=(vmem,) * len(outputs),
        compiler_params=pltpu.CompilerParams(vmem_limit_bytes=total * 256 + 2 * 2**20),
        name="rearranged",
    )(*map(in_vmem, arrays), *after)


def blank(shape, token):
    return pl.pallas_call(
        lambda token_ref, o_ref: None,
        out_shape=pltpu.HBM(shape, BF16),
        in_specs=[pl.BlockSpec(memory_space=pl.ANY)],
        out_specs=pl.BlockSpec(memory_space=pltpu.HBM),
        compiler_params=pltpu.CompilerParams(vmem_limit_bytes=2**20),
        name="blank",
    )(token)


def on_device(spectra, block_mask):
    count, segs = spectra.shape[0], spectra.shape[1]
    src_count, rcv_count = lax.axis_size("src"), lax.axis_size("rcv")
    src, rcv = lax.axis_index("src"), lax.axis_index("rcv")
    highs, steps = src_count // 2, rcv_count // 2

    def over_core(half):
        return lax.ppermute(half, "src", [(s, s ^ 1) for s in range(src_count)])

    def over_high(half):
        return lax.ppermute(half, "src", [(s, (s + 2) % src_count) for s in range(src_count)])

    def over_x(half):
        return lax.ppermute(half, "rcv", [(r, r ^ 1) for r in range(rcv_count)])

    def over_z(half):
        return lax.ppermute(half, "rcv", [(r, (r + 2) % rcv_count) for r in range(rcv_count)])

    def whole_at(array, start=0):
        return (array, start), (array, start + HALF_ROWS)

    own = prepare(spectra)
    passing = paced(over_z(own), wait_bytes=PACE)
    sources = [whole_at(own), whole_at(passing)]
    beside, high = over_x(own), over_high(own)
    cuts, ahead = [n * GROUP_ROWS for n in CUTS], []
    listed = [[(3, start, end - start)] for start, end in zip(cuts, cuts[1:])]
    mine, theirs = [whole_at(own)], [whole_at(beside)]
    if highs > 1:
        three = [(n, 0, BLOCK_ROWS) for n in range(3)]
        joined, first, second, *next_ = rearranged(
            [own, beside, high, passing],
            [three, [(1, 0, HALF_ROWS)], [(2, HALF_ROWS, HALF_ROWS)]] + (listed if steps > 2 else []),
        )
        ahead = [over_z(piece) for piece in next_]
        joined = over_core(joined)
        mine += [whole_at(joined), whole_at(high), whole_at(joined, 2 * BLOCK_ROWS)]
        theirs += [whole_at(joined, BLOCK_ROWS)]
    else:
        mine += [whole_at(over_core(own))]
        theirs += [whole_at(over_core(beside))]
    for k in range(1, highs):
        if k > 1:
            high = over_high(high)
            (second,) = rearranged([high], [[(0, HALF_ROWS, HALF_ROWS)]])
            mine += [whole_at(high), whole_at(over_core(high))]
        first, across = over_high(first), over_x(second)
        (pair,) = rearranged(
            [first, across], [[(0, 0, HALF_ROWS), (1, 0, HALF_ROWS)]], ahead[:1] if k == 1 else ()
        )
        theirs += [((first, 0), (across, 0)), whole_at(over_core(pair))]
    blocks = mine + theirs
    if len(blocks) <= 8:
        arrays, listed = [], []
        for block in blocks:
            for array, at in block:
                if not any(array is known for known in arrays):
                    arrays.append(array)
                listed.append(([array is known for known in arrays].index(True), at, HALF_ROWS))
        (together,) = rearranged(arrays, [listed], ahead[1:-1])
        blocks = [whole_at(together, n * BLOCK_ROWS) for n in range(len(blocks))]
    held = list({id(array): array for block in blocks for array, _ in block}.values())
    turn = turn_matrix()
    x, z = rcv % 2, rcv // 2
    pieces = []
    for k in range(1, steps):
        batch = sources
        if k + 1 < steps:
            early, late = ahead if k == 1 else (over_z(early), over_z(late))
        *outs, token = products(block_mask, turn, batch, blocks, count, 1.0 / math.sqrt(segs))
        if k + 2 < steps:
            late = paced(late, (token,), PACE)
        rows = [(n, 0, piece.shape[0]) for n, piece in enumerate((early, late))]
        sources = [whole_at(rearranged([early, late], [rows])[0])]
        pieces += [(kept, over_x(sent)) for kept, sent in zip(outs[::2], outs[1::2])]
    result = blank((steps, 2, count, src_count, count, 576), token)
    for k, (kept, got) in enumerate(pieces):
        at = lax.rem(z - k + steps, steps)
        result = lax.dynamic_update_slice(result, kept[None, None], (at, x, 0, 0, 0, 0))
        result = lax.dynamic_update_slice(result, got[None, None], (at, 1 - x, 0, 0, 0, 0))
    return result.reshape(steps * 2 * count, src_count, count, 576)


def solution(mesh):
    placed = (P(("src", "rcv"), None, None), P())
    return jax.shard_map(
        on_device,
        mesh=mesh,
        in_specs=placed,
        out_specs=P("src", None, "rcv", None),
        check_vma=False,
    )
```

```python
import functools
import math

import jax
import jax.numpy as jnp
import numpy as np
from jax import lax
from jax.experimental import pallas as pl
from jax.experimental.pallas import tpu as pltpu
from jax.sharding import PartitionSpec as P

GROUPS = 8
TILES = 27
PAIR_ROWS = 13 * 16
GROUP_ROWS = TILES * 16
BLOCK_ROWS = GROUPS * GROUP_ROWS
HALF_ROWS = BLOCK_ROWS // 2
STATIONS = 8
CUTS = (0, 5, 8)
PACE = 80 * 2**20
F32 = jnp.float32
BF16 = jnp.bfloat16


def prepare_kernel(x_ref, whole_ref, d_ref):
    count, segs = x_ref.shape[0], x_ref.shape[1]
    tail = segs - 256
    if count < STATIONS:
        d_ref[...] = jnp.zeros_like(d_ref)
    lane_group = lax.broadcasted_iota(jnp.int32, (8, 128), 1) // 32
    for i in range(count):
        values = x_ref[i].astype(F32)
        power = jnp.mean(values * values, axis=1, keepdims=True)
        white = (values * lax.rsqrt(power + 1e-06)).astype(BF16).astype(F32)
        main = white[:256].T
        rest = jnp.concatenate([white[256:], jnp.zeros((32 - tail, 192), F32)], axis=0)
        rest = jnp.concatenate([rest] * 4, axis=0).T
        for group in range(4):
            half, pair = group // 2, group % 2
            row = pair * PAIR_ROWS + half * 8 + i
            for line in range(6):
                rows = slice(line * 32 + group * 8, line * 32 + group * 8 + 8)
                for side in range(2):
                    tile = line * 2 + side
                    d_ref[pl.ds(row + tile * 16, 8, stride=GROUP_ROWS), :] = main[
                        rows, side * 128 : side * 128 + 128
                    ]
            first = jnp.zeros((8, 128), F32)
            for line in range(4):
                rows = slice(line * 32 + group * 8, line * 32 + group * 8 + 8)
                first = jnp.where(lane_group == line, rest[rows], first)
            d_ref[pl.ds(row + 12 * 16, 8, stride=GROUP_ROWS), :] = first
        for half in range(2):
            last = jnp.zeros((8, 128), F32)
            for pair in range(2):
                for part in range(2):
                    start = (4 + part) * 32 + (half * 2 + pair) * 8
                    last = jnp.where(
                        lane_group == pair * 2 + part, rest[start : start + 8], last
                    )
            d_ref[pl.ds(26 * 16 + half * 8 + i, 8, stride=GROUP_ROWS), :] = last
    for start in range(0, BLOCK_ROWS, 144):
        whole_ref[start : start + 144] = d_ref[start : start + 144].astype(BF16)


def in_vmem(array):
    return pltpu.with_memory_space_constraint(array, pltpu.VMEM)


def prepare(spectra):
    vmem = pl.BlockSpec(memory_space=pltpu.VMEM)
    return pl.pallas_call(
        prepare_kernel,
        out_shape=pltpu.VMEM((BLOCK_ROWS, 128), BF16),
        in_specs=[vmem],
        out_specs=vmem,
        scratch_shapes=[pltpu.VMEM((BLOCK_ROWS, 128), F32)],
        compiler_params=pltpu.CompilerParams(vmem_limit_bytes=8 * 2**20),
        name="prepare",
    )(spectra)


def turn_matrix():
    lane = np.arange(128)
    late, imag = lane // 64, lane // 32 % 2
    lines = np.stack([late == 0, late == 1, imag == 0, -imag]).astype(np.float32)
    return jnp.asarray(np.repeat(lines, 16, axis=0), BF16)


def nt(left, right):
    return lax.dot_general(left, right, (((1,), (1,)), ((), ())), preferred_element_type=F32)


def products_kernel(layout, source_count, src_count, norm, mask_ref, turn_ref, *refs):
    arrays = 1 + max(n for block in layout for n, _ in block)
    operands, outs, (token_ref, sums) = refs[:arrays], refs[arrays:-2], refs[-2:]
    token_ref[...] = jnp.zeros_like(token_ref)
    count = outs[0].shape[0]
    block_count = len(layout) - source_count
    lanes = block_count * 16
    tiles_wide = sums.shape[0] // (source_count * STATIONS * 576)
    pieces = [[(operands[n], at) for n, at in block] for block in layout]
    lefts, rights = pieces[:source_count], pieces[source_count:]
    steps = GROUPS // 2
    for h in range(2):
        def group(q, carry, h=h):
            def rows_of(ref, at, tile):
                return ref[pl.ds(pl.multiple_of(q * GROUP_ROWS + at + tile * 16, 16), 16), :]

            def tile_of(tile):
                return jnp.concatenate([rows_of(*p[h], tile) for p in rights], axis=0)

            def turned(tile):
                swapped = pltpu.roll(tile, 96, 1) * signs[2] + pltpu.roll(tile, 32, 1) * signs[3]
                lines = []
                for value in (tile, swapped):
                    across = pltpu.roll(value, 64, 1)
                    lines.append((value * signs[0], across * signs[1], across * signs[0], value * signs[1]))
                return [[line[2 * half : 2 * half + 2] for line in lines] for half in range(2)]

            signs = [turn_ref[16 * k : 16 * k + 16] for k in range(4)]
            last_right = tile_of(26)
            last_turned = [turned(rows_of(*p[h], 26)) for p in lefts]
            for pair in range(2):
                lines = []
                for p in lefts:
                    tiles = [rows_of(*p[h], pair * 13 + t) for t in range(12)]
                    for a in range(3):
                        real, imag = tiles[a * 4 : a * 4 + 2], tiles[a * 4 + 2 : a * 4 + 4]
                        lines.append(jnp.concatenate(real + imag, axis=1))
                        lines.append(jnp.concatenate(imag + [-real[0], -real[1]], axis=1))
                main = jnp.concatenate(lines, axis=0)
                rest_right = tile_of(pair * 13 + 12)
                first_turned = [turned(rows_of(*p[h], pair * 13 + 12)) for p in lefts]
                for b in range(3):
                    slot = b if b < 2 else pair
                    rest = []
                    for source in range(source_count):
                        for a in range(3):
                            of = first_turned[source][a] if a < 2 else last_turned[source][pair]
                            rest += [of[e][slot] for e in range(2)]
                    rest = jnp.concatenate(rest, axis=0)
                    weights = [tile_of(pair * 13 + b * 4 + t) for t in range(4)]
                    weights.append(rest_right if b < 2 else last_right)
                    result = nt(
                        jnp.concatenate([main, rest], axis=1), jnp.concatenate(weights, axis=1)
                    )
                    for n in range(source_count * 12):
                        source, a, e, half = n // 12, n // 4 % 3, n // 2 % 2, n % 2
                        at = (a * 6 + b * 2 + e) * 32 + half * 16 + pair * 8 + h * steps
                        for m in range(tiles_wide):
                            start = (source * tiles_wide + m) * STATIONS * 576 + at + q
                            wide = min(128, lanes)
                            sums[pl.ds(start, 8, stride=576), :wide] = result[
                                n * 8 : n * 8 + 8, m * 128 : m * 128 + wide
                            ]
            return carry

        lax.fori_loop(0, steps, group, 0, unroll=block_count <= 8)

    src = lax.axis_index("src")
    highs = src_count // 2
    places, scales = [], []
    for block in range(src_count):
        high = lax.rem(src // 2 + highs - block // 2, highs)
        places.append(high * 2 + lax.rem(src + block, 2))
        scales.append(mask_ref[src, places[-1]].astype(F32) * norm)

    bin_half = (lax.broadcasted_iota(jnp.int32, (8, 576), 1) % 32) < 16
    for source in range(source_count):
        for i in range(count):
            for m in range(tiles_wide):
                start = ((source * tiles_wide + m) * STATIONS + i) * 576
                turned = sums[start : start + 576, :].T
                for n in range(min(8, block_count)):
                    low, high = turned[n * 16 : n * 16 + 8], turned[n * 16 + 8 : n * 16 + 16]
                    which, block = divmod(m * 8 + n, src_count)
                    at = places[block]
                    value = (jnp.where(bin_half, low, high) * scales[block]).astype(BF16)
                    outs[2 * source + which][i, at] = value[: outs[0].shape[2]]


@functools.partial(jax.jit, static_argnums=(3, 4, 5, 6))
def products_of(mask, turn, operands, layout, s, count, norm):
    n = len(layout) - s
    src_count = n // 2
    sum_rows = s * ((n + 7) // 8) * STATIONS * 576
    out = jax.ShapeDtypeStruct((count, src_count, count, 576), BF16)
    smem, vmem = pl.BlockSpec(memory_space=pltpu.SMEM), pl.BlockSpec(memory_space=pltpu.VMEM)
    operands = [in_vmem(operand) for operand in operands]
    return pl.pallas_call(
        functools.partial(products_kernel, layout, s, src_count, norm),
        out_shape=(out,) * (2 * s) + (jax.ShapeDtypeStruct((8, 128), F32),),
        in_specs=[smem, vmem] + [vmem] * len(operands),
        out_specs=(vmem,) * (2 * s + 1),
        scratch_shapes=[pltpu.VMEM((sum_rows, 128), F32)],
        compiler_params=pltpu.CompilerParams(vmem_limit_bytes=2 * sum_rows // s * 512 + 12 * 2**20),
        cost_estimate=pl.CostEstimate(
            flops=2 * 16 * 3 * 96 * s * 16 * n * 768, bytes_accessed=8 * 2**20, transcendentals=0
        ),
        name="products",
    )(mask, turn, *operands)


def products(mask, turn, sources, blocks, count, norm):
    operands, layout = [], []
    for block in (*sources, *blocks):
        layout.append([])
        for array, at in block:
            known = [n for n, operand in enumerate(operands) if operand is array]
            layout[-1].append((known[0] if known else len(operands), at))
            if not known:
                operands.append(array)
    layout = tuple(map(tuple, layout))
    return products_of(mask, turn, operands, layout, len(sources), count, norm)


def paced(array, after=(), wait_bytes=0):
    any_ = pl.BlockSpec(memory_space=pl.ANY)
    return pl.pallas_call(
        lambda *refs: None,
        out_shape=pltpu.VMEM(array.shape, array.dtype),
        in_specs=[any_] * (1 + len(after)),
        out_specs=any_,
        input_output_aliases={0: 0},
        cost_estimate=pl.CostEstimate(flops=0, bytes_accessed=wait_bytes, transcendentals=0),
        compiler_params=pltpu.CompilerParams(vmem_limit_bytes=2**20),
        name="paced",
    )(in_vmem(array), *after)


def rearranged(arrays, outputs, after=()):
    def kernel(*refs):
        ins, outs = refs[: len(arrays)], refs[len(arrays) + len(after) :]
        for out_ref, pieces in zip(outs, outputs):
            at = 0
            for array, start, rows in pieces:
                for row in range(0, rows, 144):
                    out_ref[at + row : at + row + 144] = ins[array][start + row : start + row + 144]
                at += rows

    vmem = pl.BlockSpec(memory_space=pltpu.VMEM)
    sizes = [sum(rows for _, _, rows in pieces) for pieces in outputs]
    total = sum(sizes) + sum(array.shape[0] for array in arrays)
    return pl.pallas_call(
        kernel,
        out_shape=tuple(pltpu.VMEM((size, 128), BF16) for size in sizes),
        in_specs=[vmem] * len(arrays) + [pl.BlockSpec(memory_space=pl.ANY)] * len(after),
        out_specs=(vmem,) * len(outputs),
        compiler_params=pltpu.CompilerParams(vmem_limit_bytes=total * 256 + 2 * 2**20),
        name="rearranged",
    )(*map(in_vmem, arrays), *after)


def blank(shape, token):
    return pl.pallas_call(
        lambda token_ref, o_ref: None,
        out_shape=pltpu.HBM(shape, BF16),
        in_specs=[pl.BlockSpec(memory_space=pl.ANY)],
        out_specs=pl.BlockSpec(memory_space=pltpu.HBM),
        compiler_params=pltpu.CompilerParams(vmem_limit_bytes=2**20),
        name="blank",
    )(token)


def on_device(spectra, block_mask):
    count, segs = spectra.shape[0], spectra.shape[1]
    src_count, rcv_count = lax.axis_size("src"), lax.axis_size("rcv")
    src, rcv = lax.axis_index("src"), lax.axis_index("rcv")
    highs, steps = src_count // 2, rcv_count // 2

    def over_core(half):
        return lax.ppermute(half, "src", [(s, s ^ 1) for s in range(src_count)])

    def over_high(half):
        return lax.ppermute(half, "src", [(s, (s + 2) % src_count) for s in range(src_count)])

    def over_x(half):
        return lax.ppermute(half, "rcv", [(r, r ^ 1) for r in range(rcv_count)])

    ring = [*range(0, steps, 2), *reversed(range(1, steps, 2))]

    def behind(plane, k):
        return ring[(ring.index(plane) - k) % steps]

    def over_z(half):
        moves = [(behind(r // 2, 1) * 2 + r % 2, r) for r in range(rcv_count)]
        return lax.ppermute(half, "rcv", moves)

    def whole_at(array, start=0):
        return (array, start), (array, start + HALF_ROWS)

    own = prepare(spectra)
    passing = paced(over_z(own), wait_bytes=PACE)
    sources = [whole_at(own), whole_at(passing)]
    beside, high = over_x(own), over_high(own)
    cuts, ahead = [n * GROUP_ROWS for n in CUTS], []
    listed = [[(3, start, end - start)] for start, end in zip(cuts, cuts[1:])]
    mine, theirs = [whole_at(own)], [whole_at(beside)]
    if highs > 1:
        three = [(n, 0, BLOCK_ROWS) for n in range(3)]
        joined, first, second, *next_ = rearranged(
            [own, beside, high, passing],
            [three, [(1, 0, HALF_ROWS)], [(2, HALF_ROWS, HALF_ROWS)]] + (listed if steps > 2 else []),
        )
        ahead = [over_z(piece) for piece in next_]
        joined = over_core(joined)
        mine += [whole_at(joined), whole_at(high), whole_at(joined, 2 * BLOCK_ROWS)]
        theirs += [whole_at(joined, BLOCK_ROWS)]
    else:
        mine += [whole_at(over_core(own))]
        theirs += [whole_at(over_core(beside))]
    for k in range(1, highs):
        if k > 1:
            high = over_high(high)
            (second,) = rearranged([high], [[(0, HALF_ROWS, HALF_ROWS)]])
            mine += [whole_at(high), whole_at(over_core(high))]
        first, across = over_high(first), over_x(second)
        (pair,) = rearranged(
            [first, across], [[(0, 0, HALF_ROWS), (1, 0, HALF_ROWS)]], ahead[:1] if k == 1 else ()
        )
        theirs += [((first, 0), (across, 0)), whole_at(over_core(pair))]
    blocks = mine + theirs
    if len(blocks) <= 8:
        arrays, listed = [], []
        for block in blocks:
            for array, at in block:
                if not any(array is known for known in arrays):
                    arrays.append(array)
                listed.append(([array is known for known in arrays].index(True), at, HALF_ROWS))
        (together,) = rearranged(arrays, [listed], ahead[1:-1])
        blocks = [whole_at(together, n * BLOCK_ROWS) for n in range(len(blocks))]
    held = list({id(array): array for block in blocks for array, _ in block}.values())
    turn = turn_matrix()
    x, z = rcv % 2, rcv // 2
    pieces = []
    for k in range(1, steps):
        batch = sources
        if k + 1 < steps:
            early, late = ahead if k == 1 else (over_z(early), over_z(late))
        *outs, token = products(block_mask, turn, batch, blocks, count, 1.0 / math.sqrt(segs))
        if k + 2 < steps:
            late = paced(late, (token,), PACE)
        rows = [(n, 0, piece.shape[0]) for n, piece in enumerate((early, late))]
        sources = [whole_at(rearranged([early, late], [rows])[0])]
        pieces += [(kept, over_x(sent)) for kept, sent in zip(outs[::2], outs[1::2])]
    result = blank((steps, 2, count, src_count, count, 576), token)
    for k, (kept, got) in enumerate(pieces):
        at = sum(jnp.where(z == plane, behind(plane, k), 0) for plane in range(steps))
        result = lax.dynamic_update_slice(result, kept[None, None], (at, x, 0, 0, 0, 0))
        result = lax.dynamic_update_slice(result, got[None, None], (at, 1 - x, 0, 0, 0, 0))
    return result.reshape(steps * 2 * count, src_count, count, 576)


def solution(mesh):
    placed = (P(("src", "rcv"), None, None), P())
    return jax.shard_map(
        on_device,
        mesh=mesh,
        in_specs=placed,
        out_specs=P("src", None, "rcv", None),
        check_vma=False,
    )
```

```python
import functools
import math

import jax
import jax.numpy as jnp
import numpy as np
from jax import lax
from jax.experimental import pallas as pl
from jax.experimental.pallas import tpu as pltpu
from jax.sharding import PartitionSpec as P

GROUPS = 8
TILES = 27
PAIR_ROWS = 13 * 16
GROUP_ROWS = TILES * 16
BLOCK_ROWS = GROUPS * GROUP_ROWS
HALF_ROWS = BLOCK_ROWS // 2
STATIONS = 8
CUTS = (0, 1, 5, 8)
PACE = 80 * 2**20
F32 = jnp.float32
BF16 = jnp.bfloat16


def prepare_kernel(x_ref, whole_ref, d_ref):
    count, segs = x_ref.shape[0], x_ref.shape[1]
    tail = segs - 256
    if count < STATIONS:
        d_ref[...] = jnp.zeros_like(d_ref)
    lane_group = lax.broadcasted_iota(jnp.int32, (8, 128), 1) // 32
    for i in range(count):
        values = x_ref[i].astype(F32)
        power = jnp.mean(values * values, axis=1, keepdims=True)
        white = (values * lax.rsqrt(power + 1e-06)).astype(BF16).astype(F32)
        main = white[:256].T
        rest = jnp.concatenate([white[256:], jnp.zeros((32 - tail, 192), F32)], axis=0)
        rest = jnp.concatenate([rest] * 4, axis=0).T
        for group in range(4):
            half, pair = group // 2, group % 2
            row = pair * PAIR_ROWS + half * 8 + i
            for line in range(6):
                rows = slice(line * 32 + group * 8, line * 32 + group * 8 + 8)
                for side in range(2):
                    tile = line * 2 + side
                    d_ref[pl.ds(row + tile * 16, 8, stride=GROUP_ROWS), :] = main[
                        rows, side * 128 : side * 128 + 128
                    ]
            first = jnp.zeros((8, 128), F32)
            for line in range(4):
                rows = slice(line * 32 + group * 8, line * 32 + group * 8 + 8)
                first = jnp.where(lane_group == line, rest[rows], first)
            d_ref[pl.ds(row + 12 * 16, 8, stride=GROUP_ROWS), :] = first
        for half in range(2):
            last = jnp.zeros((8, 128), F32)
            for pair in range(2):
                for part in range(2):
                    start = (4 + part) * 32 + (half * 2 + pair) * 8
                    last = jnp.where(
                        lane_group == pair * 2 + part, rest[start : start + 8], last
                    )
            d_ref[pl.ds(26 * 16 + half * 8 + i, 8, stride=GROUP_ROWS), :] = last
    for start in range(0, BLOCK_ROWS, 144):
        whole_ref[start : start + 144] = d_ref[start : start + 144].astype(BF16)


def in_vmem(array):
    return pltpu.with_memory_space_constraint(array, pltpu.VMEM)


def prepare(spectra):
    vmem = pl.BlockSpec(memory_space=pltpu.VMEM)
    return pl.pallas_call(
        prepare_kernel,
        out_shape=pltpu.VMEM((BLOCK_ROWS, 128), BF16),
        in_specs=[vmem],
        out_specs=vmem,
        scratch_shapes=[pltpu.VMEM((BLOCK_ROWS, 128), F32)],
        compiler_params=pltpu.CompilerParams(vmem_limit_bytes=8 * 2**20),
        name="prepare",
    )(spectra)


def turn_matrix():
    lane = np.arange(128)
    late, imag = lane // 64, lane // 32 % 2
    lines = np.stack([late == 0, late == 1, imag == 0, -imag]).astype(np.float32)
    return jnp.asarray(np.repeat(lines, 16, axis=0), BF16)


def nt(left, right):
    return lax.dot_general(left, right, (((1,), (1,)), ((), ())), preferred_element_type=F32)


def products_kernel(layout, source_count, src_count, norm, mask_ref, turn_ref, *refs):
    arrays = 1 + max(n for block in layout for n, _ in block)
    operands, outs, (token_ref, sums) = refs[:arrays], refs[arrays:-2], refs[-2:]
    token_ref[...] = jnp.zeros_like(token_ref)
    count = outs[0].shape[0]
    block_count = len(layout) - source_count
    lanes = block_count * 16
    tiles_wide = sums.shape[0] // (source_count * STATIONS * 576)
    pieces = [[(operands[n], at) for n, at in block] for block in layout]
    lefts, rights = pieces[:source_count], pieces[source_count:]
    steps = GROUPS // 2
    for h in range(2):
        def group(q, carry, h=h):
            def rows_of(ref, at, tile):
                return ref[pl.ds(pl.multiple_of(q * GROUP_ROWS + at + tile * 16, 16), 16), :]

            def tile_of(tile):
                return jnp.concatenate([rows_of(*p[h], tile) for p in rights], axis=0)

            def turned(tile):
                swapped = pltpu.roll(tile, 96, 1) * signs[2] + pltpu.roll(tile, 32, 1) * signs[3]
                lines = []
                for value in (tile, swapped):
                    across = pltpu.roll(value, 64, 1)
                    lines.append((value * signs[0], across * signs[1], across * signs[0], value * signs[1]))
                return [[line[2 * half : 2 * half + 2] for line in lines] for half in range(2)]

            signs = [turn_ref[16 * k : 16 * k + 16] for k in range(4)]
            last_right = tile_of(26)
            last_turned = [turned(rows_of(*p[h], 26)) for p in lefts]
            for pair in range(2):
                lines = []
                for p in lefts:
                    tiles = [rows_of(*p[h], pair * 13 + t) for t in range(12)]
                    for a in range(3):
                        real, imag = tiles[a * 4 : a * 4 + 2], tiles[a * 4 + 2 : a * 4 + 4]
                        lines.append(jnp.concatenate(real + imag, axis=1))
                        lines.append(jnp.concatenate(imag + [-real[0], -real[1]], axis=1))
                main = jnp.concatenate(lines, axis=0)
                rest_right = tile_of(pair * 13 + 12)
                first_turned = [turned(rows_of(*p[h], pair * 13 + 12)) for p in lefts]
                for b in range(3):
                    slot = b if b < 2 else pair
                    rest = []
                    for source in range(source_count):
                        for a in range(3):
                            of = first_turned[source][a] if a < 2 else last_turned[source][pair]
                            rest += [of[e][slot] for e in range(2)]
                    rest = jnp.concatenate(rest, axis=0)
                    weights = [tile_of(pair * 13 + b * 4 + t) for t in range(4)]
                    weights.append(rest_right if b < 2 else last_right)
                    result = nt(
                        jnp.concatenate([main, rest], axis=1), jnp.concatenate(weights, axis=1)
                    )
                    for n in range(source_count * 12):
                        source, a, e, half = n // 12, n // 4 % 3, n // 2 % 2, n % 2
                        at = (a * 6 + b * 2 + e) * 32 + half * 16 + pair * 8 + h * steps
                        for m in range(tiles_wide):
                            start = (source * tiles_wide + m) * STATIONS * 576 + at + q
                            wide = min(128, lanes)
                            sums[pl.ds(start, 8, stride=576), :wide] = result[
                                n * 8 : n * 8 + 8, m * 128 : m * 128 + wide
                            ]
            return carry

        lax.fori_loop(0, steps, group, 0, unroll=block_count <= 8)

    src = lax.axis_index("src")
    highs = src_count // 2
    places, scales = [], []
    for block in range(src_count):
        high = lax.rem(src // 2 + highs - block // 2, highs)
        places.append(high * 2 + lax.rem(src + block, 2))
        scales.append(mask_ref[src, places[-1]].astype(F32) * norm)

    bin_half = (lax.broadcasted_iota(jnp.int32, (8, 576), 1) % 32) < 16
    for source in range(source_count):
        for i in range(count):
            for m in range(tiles_wide):
                start = ((source * tiles_wide + m) * STATIONS + i) * 576
                turned = sums[start : start + 576, :].T
                for n in range(min(8, block_count)):
                    low, high = turned[n * 16 : n * 16 + 8], turned[n * 16 + 8 : n * 16 + 16]
                    which, block = divmod(m * 8 + n, src_count)
                    at = places[block]
                    value = (jnp.where(bin_half, low, high) * scales[block]).astype(BF16)
                    outs[2 * source + which][i, at] = value[: outs[0].shape[2]]


@functools.partial(jax.jit, static_argnums=(3, 4, 5, 6))
def products_of(mask, turn, operands, layout, s, count, norm):
    n = len(layout) - s
    src_count = n // 2
    sum_rows = s * ((n + 7) // 8) * STATIONS * 576
    out = jax.ShapeDtypeStruct((count, src_count, count, 576), BF16)
    smem, vmem = pl.BlockSpec(memory_space=pltpu.SMEM), pl.BlockSpec(memory_space=pltpu.VMEM)
    operands = [in_vmem(operand) for operand in operands]
    return pl.pallas_call(
        functools.partial(products_kernel, layout, s, src_count, norm),
        out_shape=(out,) * (2 * s) + (jax.ShapeDtypeStruct((8, 128), F32),),
        in_specs=[smem, vmem] + [vmem] * len(operands),
        out_specs=(vmem,) * (2 * s + 1),
        scratch_shapes=[pltpu.VMEM((sum_rows, 128), F32)],
        compiler_params=pltpu.CompilerParams(vmem_limit_bytes=2 * sum_rows // s * 512 + 12 * 2**20),
        cost_estimate=pl.CostEstimate(
            flops=2 * 16 * 3 * 96 * s * 16 * n * 768, bytes_accessed=8 * 2**20, transcendentals=0
        ),
        name="products",
    )(mask, turn, *operands)


def products(mask, turn, sources, blocks, count, norm):
    operands, layout = [], []
    for block in (*sources, *blocks):
        layout.append([])
        for array, at in block:
            known = [n for n, operand in enumerate(operands) if operand is array]
            layout[-1].append((known[0] if known else len(operands), at))
            if not known:
                operands.append(array)
    layout = tuple(map(tuple, layout))
    return products_of(mask, turn, operands, layout, len(sources), count, norm)


def paced(array, after=(), wait_bytes=0):
    any_ = pl.BlockSpec(memory_space=pl.ANY)
    return pl.pallas_call(
        lambda *refs: None,
        out_shape=pltpu.VMEM(array.shape, array.dtype),
        in_specs=[any_] * (1 + len(after)),
        out_specs=any_,
        input_output_aliases={0: 0},
        cost_estimate=pl.CostEstimate(flops=0, bytes_accessed=wait_bytes, transcendentals=0),
        compiler_params=pltpu.CompilerParams(vmem_limit_bytes=2**20),
        name="paced",
    )(in_vmem(array), *after)


def rearranged(arrays, outputs, after=()):
    def kernel(*refs):
        ins, outs = refs[: len(arrays)], refs[len(arrays) + len(after) :]
        for out_ref, pieces in zip(outs, outputs):
            at = 0
            for array, start, rows in pieces:
                for row in range(0, rows, 144):
                    out_ref[at + row : at + row + 144] = ins[array][start + row : start + row + 144]
                at += rows

    vmem = pl.BlockSpec(memory_space=pltpu.VMEM)
    sizes = [sum(rows for _, _, rows in pieces) for pieces in outputs]
    total = sum(sizes) + sum(array.shape[0] for array in arrays)
    return pl.pallas_call(
        kernel,
        out_shape=tuple(pltpu.VMEM((size, 128), BF16) for size in sizes),
        in_specs=[vmem] * len(arrays) + [pl.BlockSpec(memory_space=pl.ANY)] * len(after),
        out_specs=(vmem,) * len(outputs),
        compiler_params=pltpu.CompilerParams(vmem_limit_bytes=total * 256 + 2 * 2**20),
        name="rearranged",
    )(*map(in_vmem, arrays), *after)


def blank(shape, token):
    return pl.pallas_call(
        lambda token_ref, o_ref: None,
        out_shape=pltpu.HBM(shape, BF16),
        in_specs=[pl.BlockSpec(memory_space=pl.ANY)],
        out_specs=pl.BlockSpec(memory_space=pltpu.HBM),
        compiler_params=pltpu.CompilerParams(vmem_limit_bytes=2**20),
        name="blank",
    )(token)


def on_device(spectra, block_mask):
    count, segs = spectra.shape[0], spectra.shape[1]
    src_count, rcv_count = lax.axis_size("src"), lax.axis_size("rcv")
    src, rcv = lax.axis_index("src"), lax.axis_index("rcv")
    highs, steps = src_count // 2, rcv_count // 2

    def over_core(half):
        return lax.ppermute(half, "src", [(s, s ^ 1) for s in range(src_count)])

    def over_high(half):
        return lax.ppermute(half, "src", [(s, (s + 2) % src_count) for s in range(src_count)])

    def over_x(half):
        return lax.ppermute(half, "rcv", [(r, r ^ 1) for r in range(rcv_count)])

    ring = [*range(0, steps, 2), *reversed(range(1, steps, 2))]

    def behind(plane, k):
        return ring[(ring.index(plane) - k) % steps]

    def over_z(half):
        moves = [(behind(r // 2, 1) * 2 + r % 2, r) for r in range(rcv_count)]
        return lax.ppermute(half, "rcv", moves)

    def whole_at(array, start=0):
        return (array, start), (array, start + HALF_ROWS)

    own = prepare(spectra)
    passing = paced(over_z(own), wait_bytes=PACE)
    sources = [whole_at(own), whole_at(passing)]
    beside, high = over_x(own), over_high(own)
    cuts, ahead = [n * GROUP_ROWS for n in CUTS], []
    if steps > 2:
        listed = [[(0, start, end - start)] for start, end in zip(cuts, cuts[1:])]
        ahead = [over_z(piece) for piece in rearranged([passing], listed)]
    mine, theirs = [whole_at(own)], [whole_at(beside)]
    if highs > 1:
        three = [(n, 0, BLOCK_ROWS) for n in range(3)]
        joined, first, second = rearranged(
            [own, beside, high],
            [three, [(1, 0, HALF_ROWS)], [(2, HALF_ROWS, HALF_ROWS)]],
            (passing, *ahead[:1]),
        )
        joined = over_core(joined)
        mine += [whole_at(joined), whole_at(high), whole_at(joined, 2 * BLOCK_ROWS)]
        theirs += [whole_at(joined, BLOCK_ROWS)]
    else:
        mine += [whole_at(over_core(own))]
        theirs += [whole_at(over_core(beside))]
    for k in range(1, highs):
        if k > 1:
            high = over_high(high)
            (second,) = rearranged([high], [[(0, HALF_ROWS, HALF_ROWS)]])
            mine += [whole_at(high), whole_at(over_core(high))]
        first, across = over_high(first), over_x(second)
        (pair,) = rearranged(
            [first, across], [[(0, 0, HALF_ROWS), (1, 0, HALF_ROWS)]], ahead[1:2] if k == 1 else ()
        )
        theirs += [((first, 0), (across, 0)), whole_at(over_core(pair))]
    blocks = mine + theirs
    if len(blocks) <= 8:
        arrays, listed = [], []
        for block in blocks:
            for array, at in block:
                if not any(array is known for known in arrays):
                    arrays.append(array)
                listed.append(([array is known for known in arrays].index(True), at, HALF_ROWS))
        (together,) = rearranged(arrays, [listed])
        blocks = [whole_at(together, n * BLOCK_ROWS) for n in range(len(blocks))]
    held = list({id(array): array for block in blocks for array, _ in block}.values())
    turn = turn_matrix()
    x, z = rcv % 2, rcv // 2
    pieces = []
    for k in range(1, steps):
        batch = sources
        if k + 1 < steps:
            if k == 1:
                rows = [(n, 0, piece.shape[0]) for n, piece in enumerate(ahead[:2])]
                (early,), late = rearranged(ahead[:2], [rows]), ahead[2]
            else:
                early, late = over_z(early), over_z(late)
        *outs, token = products(block_mask, turn, batch, blocks, count, 1.0 / math.sqrt(segs))
        if k + 2 < steps:
            late = paced(late, (token,), PACE)
        rows = [(n, 0, piece.shape[0]) for n, piece in enumerate((early, late))]
        sources = [whole_at(rearranged([early, late], [rows])[0])]
        pieces += [(kept, over_x(sent)) for kept, sent in zip(outs[::2], outs[1::2])]
    result = blank((steps, 2, count, src_count, count, 576), token)
    for k, (kept, got) in enumerate(pieces):
        at = sum(jnp.where(z == plane, behind(plane, k), 0) for plane in range(steps))
        result = lax.dynamic_update_slice(result, kept[None, None], (at, x, 0, 0, 0, 0))
        result = lax.dynamic_update_slice(result, got[None, None], (at, 1 - x, 0, 0, 0, 0))
    return result.reshape(steps * 2 * count, src_count, count, 576)


def solution(mesh):
    placed = (P(("src", "rcv"), None, None), P())
    return jax.shard_map(
        on_device,
        mesh=mesh,
        in_specs=placed,
        out_specs=P("src", None, "rcv", None),
        check_vma=False,
    )
```

```python
import functools
import math

import jax
import jax.numpy as jnp
import numpy as np
from jax import lax
from jax.experimental import pallas as pl
from jax.experimental.pallas import tpu as pltpu
from jax.sharding import PartitionSpec as P

GROUPS = 8
TILES = 27
PAIR_ROWS = 13 * 16
GROUP_ROWS = TILES * 16
BLOCK_ROWS = GROUPS * GROUP_ROWS
HALF_ROWS = BLOCK_ROWS // 2
STATIONS = 8
CUTS = (0, 4, 8)
PACE = 80 * 2**20
F32 = jnp.float32
BF16 = jnp.bfloat16


def prepare_kernel(x_ref, whole_ref, d_ref):
    count, segs = x_ref.shape[0], x_ref.shape[1]
    tail = segs - 256
    if count < STATIONS:
        d_ref[...] = jnp.zeros_like(d_ref)
    lane_group = lax.broadcasted_iota(jnp.int32, (8, 128), 1) // 32
    for i in range(count):
        values = x_ref[i].astype(F32)
        power = jnp.mean(values * values, axis=1, keepdims=True)
        white = (values * lax.rsqrt(power + 1e-06)).astype(BF16).astype(F32)
        main = white[:256].T
        rest = jnp.concatenate([white[256:], jnp.zeros((32 - tail, 192), F32)], axis=0)
        rest = jnp.concatenate([rest] * 4, axis=0).T
        for group in range(4):
            half, pair = group // 2, group % 2
            row = pair * PAIR_ROWS + half * 8 + i
            for line in range(6):
                rows = slice(line * 32 + group * 8, line * 32 + group * 8 + 8)
                for side in range(2):
                    tile = line * 2 + side
                    d_ref[pl.ds(row + tile * 16, 8, stride=GROUP_ROWS), :] = main[
                        rows, side * 128 : side * 128 + 128
                    ]
            first = jnp.zeros((8, 128), F32)
            for line in range(4):
                rows = slice(line * 32 + group * 8, line * 32 + group * 8 + 8)
                first = jnp.where(lane_group == line, rest[rows], first)
            d_ref[pl.ds(row + 12 * 16, 8, stride=GROUP_ROWS), :] = first
        for half in range(2):
            last = jnp.zeros((8, 128), F32)
            for pair in range(2):
                for part in range(2):
                    start = (4 + part) * 32 + (half * 2 + pair) * 8
                    last = jnp.where(
                        lane_group == pair * 2 + part, rest[start : start + 8], last
                    )
            d_ref[pl.ds(26 * 16 + half * 8 + i, 8, stride=GROUP_ROWS), :] = last
    for start in range(0, BLOCK_ROWS, 144):
        whole_ref[start : start + 144] = d_ref[start : start + 144].astype(BF16)


def in_vmem(array):
    return pltpu.with_memory_space_constraint(array, pltpu.VMEM)


def prepare(spectra):
    vmem = pl.BlockSpec(memory_space=pltpu.VMEM)
    return pl.pallas_call(
        prepare_kernel,
        out_shape=pltpu.VMEM((BLOCK_ROWS, 128), BF16),
        in_specs=[vmem],
        out_specs=vmem,
        scratch_shapes=[pltpu.VMEM((BLOCK_ROWS, 128), F32)],
        compiler_params=pltpu.CompilerParams(vmem_limit_bytes=8 * 2**20),
        name="prepare",
    )(spectra)


def turn_matrix():
    lane = np.arange(128)
    late, imag = lane // 64, lane // 32 % 2
    lines = np.stack([late == 0, late == 1, imag == 0, -imag]).astype(np.float32)
    return jnp.asarray(np.repeat(lines, 16, axis=0), BF16)


def nt(left, right):
    return lax.dot_general(left, right, (((1,), (1,)), ((), ())), preferred_element_type=F32)


def products_kernel(layout, source_count, src_count, norm, mask_ref, turn_ref, *refs):
    arrays = 1 + max(n for block in layout for n, _ in block)
    operands, outs, (token_ref, sums) = refs[:arrays], refs[arrays:-2], refs[-2:]
    token_ref[...] = jnp.zeros_like(token_ref)
    count = outs[0].shape[0]
    block_count = len(layout) - source_count
    lanes = block_count * 16
    tiles_wide = sums.shape[0] // (source_count * STATIONS * 576)
    pieces = [[(operands[n], at) for n, at in block] for block in layout]
    lefts, rights = pieces[:source_count], pieces[source_count:]
    steps = GROUPS // 2
    for h in range(2):
        def group(q, carry, h=h):
            def rows_of(ref, at, tile):
                return ref[pl.ds(pl.multiple_of(q * GROUP_ROWS + at + tile * 16, 16), 16), :]

            def tile_of(tile):
                return jnp.concatenate([rows_of(*p[h], tile) for p in rights], axis=0)

            def turned(tile):
                swapped = pltpu.roll(tile, 96, 1) * signs[2] + pltpu.roll(tile, 32, 1) * signs[3]
                lines = []
                for value in (tile, swapped):
                    across = pltpu.roll(value, 64, 1)
                    lines.append((value * signs[0], across * signs[1], across * signs[0], value * signs[1]))
                return [[line[2 * half : 2 * half + 2] for line in lines] for half in range(2)]

            signs = [turn_ref[16 * k : 16 * k + 16] for k in range(4)]
            last_right = tile_of(26)
            last_turned = [turned(rows_of(*p[h], 26)) for p in lefts]
            for pair in range(2):
                lines = []
                for p in lefts:
                    tiles = [rows_of(*p[h], pair * 13 + t) for t in range(12)]
                    for a in range(3):
                        real, imag = tiles[a * 4 : a * 4 + 2], tiles[a * 4 + 2 : a * 4 + 4]
                        lines.append(jnp.concatenate(real + imag, axis=1))
                        lines.append(jnp.concatenate(imag + [-real[0], -real[1]], axis=1))
                main = jnp.concatenate(lines, axis=0)
                rest_right = tile_of(pair * 13 + 12)
                first_turned = [turned(rows_of(*p[h], pair * 13 + 12)) for p in lefts]
                for b in range(3):
                    slot = b if b < 2 else pair
                    rest = []
                    for source in range(source_count):
                        for a in range(3):
                            of = first_turned[source][a] if a < 2 else last_turned[source][pair]
                            rest += [of[e][slot] for e in range(2)]
                    rest = jnp.concatenate(rest, axis=0)
                    weights = [tile_of(pair * 13 + b * 4 + t) for t in range(4)]
                    weights.append(rest_right if b < 2 else last_right)
                    result = nt(
                        jnp.concatenate([main, rest], axis=1), jnp.concatenate(weights, axis=1)
                    )
                    for n in range(source_count * 12):
                        source, a, e, half = n // 12, n // 4 % 3, n // 2 % 2, n % 2
                        at = (a * 6 + b * 2 + e) * 32 + half * 16 + pair * 8 + h * steps
                        for m in range(tiles_wide):
                            start = (source * tiles_wide + m) * STATIONS * 576 + at + q
                            wide = min(128, lanes)
                            sums[pl.ds(start, 8, stride=576), :wide] = result[
                                n * 8 : n * 8 + 8, m * 128 : m * 128 + wide
                            ]
            return carry

        lax.fori_loop(0, steps, group, 0, unroll=block_count <= 8)

    src = lax.axis_index("src")
    highs = src_count // 2
    places, scales = [], []
    for block in range(src_count):
        high = lax.rem(src // 2 + highs - block // 2, highs)
        places.append(high * 2 + lax.rem(src + block, 2))
        scales.append(mask_ref[src, places[-1]].astype(F32) * norm)

    bin_half = (lax.broadcasted_iota(jnp.int32, (8, 576), 1) % 32) < 16
    for source in range(source_count):
        for i in range(count):
            for m in range(tiles_wide):
                start = ((source * tiles_wide + m) * STATIONS + i) * 576
                turned = sums[start : start + 576, :].T
                for n in range(min(8, block_count)):
                    low, high = turned[n * 16 : n * 16 + 8], turned[n * 16 + 8 : n * 16 + 16]
                    which, block = divmod(m * 8 + n, src_count)
                    at = places[block]
                    value = (jnp.where(bin_half, low, high) * scales[block]).astype(BF16)
                    outs[2 * source + which][i, at] = value[: outs[0].shape[2]]


@functools.partial(jax.jit, static_argnums=(3, 4, 5, 6))
def products_of(mask, turn, operands, layout, s, count, norm):
    n = len(layout) - s
    src_count = n // 2
    sum_rows = s * ((n + 7) // 8) * STATIONS * 576
    out = jax.ShapeDtypeStruct((count, src_count, count, 576), BF16)
    smem, vmem = pl.BlockSpec(memory_space=pltpu.SMEM), pl.BlockSpec(memory_space=pltpu.VMEM)
    operands = [in_vmem(operand) for operand in operands]
    return pl.pallas_call(
        functools.partial(products_kernel, layout, s, src_count, norm),
        out_shape=(out,) * (2 * s) + (jax.ShapeDtypeStruct((8, 128), F32),),
        in_specs=[smem, vmem] + [vmem] * len(operands),
        out_specs=(vmem,) * (2 * s + 1),
        scratch_shapes=[pltpu.VMEM((sum_rows, 128), F32)],
        compiler_params=pltpu.CompilerParams(vmem_limit_bytes=2 * sum_rows // s * 512 + 12 * 2**20),
        cost_estimate=pl.CostEstimate(
            flops=2 * 16 * 3 * 96 * s * 16 * n * 768, bytes_accessed=8 * 2**20, transcendentals=0
        ),
        name="products",
    )(mask, turn, *operands)


def products(mask, turn, sources, blocks, count, norm):
    operands, layout = [], []
    for block in (*sources, *blocks):
        layout.append([])
        for array, at in block:
            known = [n for n, operand in enumerate(operands) if operand is array]
            layout[-1].append((known[0] if known else len(operands), at))
            if not known:
                operands.append(array)
    layout = tuple(map(tuple, layout))
    return products_of(mask, turn, operands, layout, len(sources), count, norm)


def paced(array, after=(), wait_bytes=0):
    any_ = pl.BlockSpec(memory_space=pl.ANY)
    return pl.pallas_call(
        lambda *refs: None,
        out_shape=pltpu.VMEM(array.shape, array.dtype),
        in_specs=[any_] * (1 + len(after)),
        out_specs=any_,
        input_output_aliases={0: 0},
        cost_estimate=pl.CostEstimate(flops=0, bytes_accessed=wait_bytes, transcendentals=0),
        compiler_params=pltpu.CompilerParams(vmem_limit_bytes=2**20),
        name="paced",
    )(in_vmem(array), *after)


def rearranged(arrays, outputs, after=()):
    def kernel(*refs):
        ins, outs = refs[: len(arrays)], refs[len(arrays) + len(after) :]
        for out_ref, pieces in zip(outs, outputs):
            at = 0
            for array, start, rows in pieces:
                for row in range(0, rows, 144):
                    out_ref[at + row : at + row + 144] = ins[array][start + row : start + row + 144]
                at += rows

    vmem = pl.BlockSpec(memory_space=pltpu.VMEM)
    sizes = [sum(rows for _, _, rows in pieces) for pieces in outputs]
    total = sum(sizes) + sum(array.shape[0] for array in arrays)
    return pl.pallas_call(
        kernel,
        out_shape=tuple(pltpu.VMEM((size, 128), BF16) for size in sizes),
        in_specs=[vmem] * len(arrays) + [pl.BlockSpec(memory_space=pl.ANY)] * len(after),
        out_specs=(vmem,) * len(outputs),
        compiler_params=pltpu.CompilerParams(vmem_limit_bytes=total * 256 + 2 * 2**20),
        name="rearranged",
    )(*map(in_vmem, arrays), *after)


def blank(shape, token):
    return pl.pallas_call(
        lambda token_ref, o_ref: None,
        out_shape=pltpu.HBM(shape, BF16),
        in_specs=[pl.BlockSpec(memory_space=pl.ANY)],
        out_specs=pl.BlockSpec(memory_space=pltpu.HBM),
        compiler_params=pltpu.CompilerParams(vmem_limit_bytes=2**20),
        name="blank",
    )(token)


def on_device(spectra, block_mask):
    count, segs = spectra.shape[0], spectra.shape[1]
    src_count, rcv_count = lax.axis_size("src"), lax.axis_size("rcv")
    src, rcv = lax.axis_index("src"), lax.axis_index("rcv")
    highs, steps = src_count // 2, rcv_count // 2

    def over_core(half):
        return lax.ppermute(half, "src", [(s, s ^ 1) for s in range(src_count)])

    def over_high(half):
        return lax.ppermute(half, "src", [(s, (s + 2) % src_count) for s in range(src_count)])

    def over_x(half):
        return lax.ppermute(half, "rcv", [(r, r ^ 1) for r in range(rcv_count)])

    ring = [*range(0, steps, 2), *reversed(range(1, steps, 2))]

    def behind(plane, k):
        return ring[(ring.index(plane) - k) % steps]

    def over_z(half):
        moves = [(behind(r // 2, 1) * 2 + r % 2, r) for r in range(rcv_count)]
        return lax.ppermute(half, "rcv", moves)

    def whole_at(array, start=0):
        return (array, start), (array, start + HALF_ROWS)

    own = prepare(spectra)
    passing = paced(over_z(own), wait_bytes=PACE)
    sources = [whole_at(own), whole_at(passing)]
    beside, high = over_x(own), over_high(own)
    cuts, ahead = [n * GROUP_ROWS for n in CUTS], []
    listed = [[(3, start, end - start)] for start, end in zip(cuts, cuts[1:])]
    mine, theirs = [whole_at(own)], [whole_at(beside)]
    if highs > 1:
        three = [(n, 0, BLOCK_ROWS) for n in range(3)]
        joined, first, second, *next_ = rearranged(
            [own, beside, high, passing],
            [three, [(1, 0, HALF_ROWS)], [(2, HALF_ROWS, HALF_ROWS)]] + (listed if steps > 2 else []),
        )
        ahead = [over_z(piece) for piece in next_]
        joined = over_core(joined)
        mine += [whole_at(joined), whole_at(high), whole_at(joined, 2 * BLOCK_ROWS)]
        theirs += [whole_at(joined, BLOCK_ROWS)]
    else:
        mine += [whole_at(over_core(own))]
        theirs += [whole_at(over_core(beside))]
    for k in range(1, highs):
        if k > 1:
            high = over_high(high)
            (second,) = rearranged([high], [[(0, HALF_ROWS, HALF_ROWS)]])
            mine += [whole_at(high), whole_at(over_core(high))]
        first, across = over_high(first), over_x(second)
        (pair,) = rearranged(
            [first, across], [[(0, 0, HALF_ROWS), (1, 0, HALF_ROWS)]], ahead[:1] if k == 1 else ()
        )
        theirs += [((first, 0), (across, 0)), whole_at(over_core(pair))]
    blocks = mine + theirs
    if len(blocks) <= 8:
        arrays, listed = [], []
        for block in blocks:
            for array, at in block:
                if not any(array is known for known in arrays):
                    arrays.append(array)
                listed.append(([array is known for known in arrays].index(True), at, HALF_ROWS))
        (together,) = rearranged(arrays, [listed], ahead[1:-1])
        blocks = [whole_at(together, n * BLOCK_ROWS) for n in range(len(blocks))]
    held = list({id(array): array for block in blocks for array, _ in block}.values())
    turn = turn_matrix()
    x, z = rcv % 2, rcv // 2
    pieces = []
    for k in range(1, steps):
        batch = sources
        if k + 1 < steps:
            early, late = ahead if k == 1 else (over_z(early), over_z(late))
        *outs, token = products(block_mask, turn, batch, blocks, count, 1.0 / math.sqrt(segs))
        if k + 2 < steps:
            late = paced(late, (token,), PACE)
        rows = [(n, 0, piece.shape[0]) for n, piece in enumerate((early, late))]
        sources = [whole_at(rearranged([early, late], [rows])[0])]
        pieces += [(kept, over_x(sent)) for kept, sent in zip(outs[::2], outs[1::2])]
    result = blank((steps, 2, count, src_count, count, 576), token)
    for k, (kept, got) in enumerate(pieces):
        at = sum(jnp.where(z == plane, behind(plane, k), 0) for plane in range(steps))
        result = lax.dynamic_update_slice(result, kept[None, None], (at, x, 0, 0, 0, 0))
        result = lax.dynamic_update_slice(result, got[None, None], (at, 1 - x, 0, 0, 0, 0))
    return result.reshape(steps * 2 * count, src_count, count, 576)


def solution(mesh):
    placed = (P(("src", "rcv"), None, None), P())
    return jax.shard_map(
        on_device,
        mesh=mesh,
        in_specs=placed,
        out_specs=P("src", None, "rcv", None),
        check_vma=False,
    )
```
